32 devices in a mesh: rep: 2 (over y), col: 4 (over z), row: 2 (over x), sub: 2 (over core).
Axes of the slice: x: 2, y: 2, z: 4, core: 2. Of those that a mesh axis runs over, the one named last changes fastest.
Arguments:
- node_query: bfloat16 [512, 256], P(('rep', 'row')), parts along dimension 0, may hold values from -6 to 6
- query_angles: float32 [3, 512], P(None, ('rep', 'row')), parts along dimension 1, may hold values from -3.140625 to 3.140625
- query_trans: float32 [3, 512], P(None, ('rep', 'row')), parts along dimension 1, may hold values from -12 to 26
- query_chain: int32 [512], P(('rep', 'row')), parts along dimension 0, may hold values from 0 to 3
- node_key: bfloat16 [2048, 256], P(('rep', 'col', 'row', 'sub')), parts along dimension 0, may hold values from -6 to 6
- key_angles: float32 [3, 2048], P(None, ('rep', 'col')), parts along dimension 1, may hold values from -3.140625 to 3.140625
- key_trans: float32 [3, 2048], P(None, ('rep', 'col')), parts along dimension 1, may hold values from -12 to 12
- key_chain: int32 [2048], P(('rep', 'col')), parts along dimension 0, may hold values from 0 to 3, never falling along the last dimension, each value on 1 to 512 neighbouring positions
- pair_features: bfloat16 [128, 512, 1024], P('sub', ('rep', 'row'), 'col'), parts along dimension 1, may hold values from -6 to 6
- pair_mask: int32 [512, 1024], P(('rep', 'row'), 'col'), parts along dimension 0, may hold values 0 or 1
- query_weight: bfloat16 [256, 336], P(None, 'sub'), may hold values from -0.375 to 0.375
- key_weight: bfloat16 [256, 816], P(None, 'sub'), may hold values from -0.375 to 0.375
- bias_weight: bfloat16 [128, 12], P(None, 'sub'), may hold values from -0.5 to 0.5
- point_gain: float32 [12], P('sub'), may hold values from 0.25 to 2
- chain_gain: float32 [12], P('sub'), may hold values from -2 to 2
- out_weight: bfloat16 [2112, 256], P('sub'), may hold values from -0.125 to 0.125
- first_gain: float32 [256], replicated, may hold values from 0.5 to 1.5
- second_gain: float32 [256], replicated, may hold values from 0.5 to 1.5
- gate_weight: bfloat16 [256, 1024], replicated, may hold values from -0.375 to 0.375
- up_weight: bfloat16 [256, 1024], replicated, may hold values from -0.375 to 0.375
- down_weight: bfloat16 [1024, 256], replicated, may hold values from -0.1875 to 0.1875
- edge_query_weight: bfloat16 [256, 256], replicated, may hold values from -0.375 to 0.375
- edge_key_weight: bfloat16 [256, 256], replicated, may hold values from -0.375 to 0.375
- edge_in_weight: bfloat16 [128, 256], replicated, may hold values from -0.5 to 0.5
- edge_out_weight: bfloat16 [256, 128], replicated, may hold values from -0.375 to 0.375
Outputs:
- updated_nodes: bfloat16 [512, 256], P(('rep', 'row')), parts along dimension 0
- updated_pairs: bfloat16 [128, 512, 1024], P('sub', ('rep', 'row'), 'col'), parts along dimension 1
The draws below stay inside these ranges and needn't reach their ends.
There are 2 independent parts, one for each index of `rep`. The reference program is written for one: setup_inputs(seed, part) draws one part's arguments, and reference() takes and returns one part's arrays. A program takes and returns all parts, laid end to end along the dimension named above; an argument that names none is the same for every part. Nothing has to cross between parts.
All inputs are finite; a program needn't handle non-finite values. No bound on the sum of `pair_mask` on one device may be relied on, other than what follows from the above.
Results may differ from the reference program's by a relative error of at most 0.006.
Values may be sent and summed in bfloat16 or wider, within the bound.
No kernel may reach another device: no remote copies, remote signals or barrier semaphores. Data moves between devices by JAX's collectives and lax.ppermute only.
A program may use at most 128 MiB of HBM per device.

```python
import math
import jax
import jax.numpy as jnp
import numpy as np
from jax import lax

CS = 256
CZ = 128
H = 12
CH = 16
PQ = 4
PV = 8
FFN = 1024
EH = 256
NCHAIN = 4
QROWS = 256
KEYS = 1024


def draw_query_trans(key, part):
    return jnp.clip(3.0 * jax.random.normal(key, (3, QROWS), jnp.float32), -12.0, 12.0)


def plant(values, rng, low, largest):
    extent = values.shape
    spot = [jax.random.randint(jax.random.fold_in(rng, axis), (), 0, extent[axis]) for axis in range(len(extent))]
    values = values.at[tuple(spot)].set(low)
    longest = extent.index(max(extent))
    spot[longest] = (spot[longest] + 1) % extent[longest]
    return values.at[tuple(spot)].set(largest)


def levels(own_key, shape, shards, low, top_value):
    level = 1.0
    for axis_at, blocks in shards:
        heights = jax.random.uniform(jax.random.fold_in(jax.random.fold_in(own_key, 6), axis_at), (blocks,), jnp.float32, low / len(shards), top_value / len(shards))
        level = level * jnp.repeat(jnp.exp(heights), shape[axis_at] // blocks).reshape((-1,) + (1,) * (len(shape) - 1 - axis_at))
    return level


def profile(amount, total, limit, slope):
    portions = [(1 << 20) // math.isqrt(standing ** slope) + 1 for standing in range(2, amount + 1)]
    spare, holding = total - limit - (amount - 1), [1] * (amount - 1)
    while spare > 0:
        candidates = [i for i in range(amount - 1) if holding[i] < limit]
        pool, remaining = sum([portions[i] for i in candidates]), spare
        for i in candidates:
            addition = min(limit - holding[i], max(1, remaining * portions[i] // pool), spare)
            holding[i] = holding[i] + addition
            spare = spare - addition
    return np.array([limit] + holding)


def ragged_sizes(key, count, total, limit, skew):
    if count == 2:
        one = jax.random.randint(key, (), max(1, total - limit), min(limit, total - 1) + 1)
        return jnp.stack([one, total - one])
    sizes = jnp.asarray(profile(count, total, limit, skew), jnp.int32)
    pairs = (count - 1) // 2
    donor, sink = sizes[1:1 + 2 * pairs:2], sizes[2:2 + 2 * pairs:2]
    slack = jnp.minimum(donor - 1, limit - sink)
    shifted = jax.random.randint(jax.random.fold_in(key, 1), (pairs,), 0, 1 << 20) % (slack + 1)
    sizes = sizes.at[1:1 + 2 * pairs:2].set(donor - shifted).at[2:2 + 2 * pairs:2].set(sink + shifted)
    return sizes[jax.random.permutation(jax.random.fold_in(key, 2), count)]


def normal_values(rng, extent, deviation, limit, split=(), kind=jnp.bfloat16):
    result = deviation * jax.random.normal(rng, extent, jnp.float32)
    if split:
        result = result * levels(rng, extent, split, -0.22, 0.18)
    return jnp.clip(result, -limit, limit).astype(kind)


def setup_inputs(seed: int = 0, part: int = 0) -> dict:
    splits = jax.random.split(jax.random.key(seed), 26)
    own_keys = jax.random.split(jax.random.fold_in(splits[25], part), 26)
    return {
        "node_query": normal_values(own_keys[0], (QROWS, CS), 1.0, 6.0, ((0, 2),)),
        "query_angles": jnp.clip(jax.random.uniform(own_keys[1], (3, QROWS), jnp.float32, -3.140625, 3.140625), -3.140625, 3.140625),
        "query_trans": draw_query_trans(jax.random.fold_in(jax.random.fold_in(splits[25], part), 71), part),
        "query_chain": plant(jax.random.randint(own_keys[3], (QROWS,), 0, NCHAIN), jax.random.fold_in(own_keys[3], 1), 0, NCHAIN - 1).astype(jnp.int32),
        "node_key": normal_values(own_keys[4], (KEYS, CS), 1.0, 6.0, ((0, 16),)),
        "key_angles": jnp.clip(jax.random.uniform(own_keys[5], (3, KEYS), jnp.float32, -3.140625, 3.140625), -3.140625, 3.140625),
        "key_trans": normal_values(own_keys[6], (3, KEYS), 3.0, 12.0, ((1, 4),), jnp.float32),
        "key_chain": jnp.searchsorted(jnp.cumsum(ragged_sizes(own_keys[7], NCHAIN, KEYS, KEYS // 2, 0)), jnp.arange(KEYS), side="right").astype(jnp.int32),
        "pair_features": normal_values(own_keys[8], (CZ, QROWS, KEYS), 1.0, 6.0, ((0, 2), (1, 2), (2, 4))),
        "pair_mask": plant((jax.random.randint(own_keys[9], (QROWS, KEYS), 0, 8) < 7).astype(jnp.int32), jax.random.fold_in(own_keys[9], 1), 0, 1),
        "query_weight": normal_values(splits[10], (CS, H * (CH + 3 * PQ)), CS ** -0.5, 0.375, ((1, 2),)),
        "key_weight": normal_values(splits[11], (CS, H * (2 * CH + 3 * PQ + 3 * PV)), CS ** -0.5, 0.375, ((1, 2),)),
        "bias_weight": normal_values(splits[12], (CZ, H), CZ ** -0.5, 0.5, ((1, 2),)),
        "point_gain": jnp.clip(jnp.exp(math.log(2.0) - 2.0794415 * jax.random.uniform(splits[13], (H,), jnp.float32) ** levels(splits[13], (H,), ((0, 2),), -0.2, 0.2)), 0.25, 2.0),
        "chain_gain": jnp.clip(jax.random.uniform(splits[14], (H,), jnp.float32, -2.0, 2.0) * levels(splits[14], (H,), ((0, 2),), -0.4, 0.0), -2.0, 2.0),
        "out_weight": normal_values(splits[15], (H * (CH + 4 * PV + CZ), CS), (H * (CH + 4 * PV + CZ)) ** -0.5, 0.125, ((0, 2),)),
        "first_gain": jnp.clip(1.0 + 0.1 * jax.random.normal(splits[16], (CS,), jnp.float32), 0.5, 1.5),
        "second_gain": jnp.clip(1.0 + 0.1 * jax.random.normal(splits[17], (CS,), jnp.float32), 0.5, 1.5),
        "gate_weight": normal_values(splits[18], (CS, FFN), CS ** -0.5, 0.375),
        "up_weight": normal_values(splits[19], (CS, FFN), CS ** -0.5, 0.375),
        "down_weight": normal_values(splits[20], (FFN, CS), FFN ** -0.5, 0.1875),
        "edge_query_weight": normal_values(splits[21], (CS, EH), CS ** -0.5, 0.375),
        "edge_key_weight": normal_values(splits[22], (CS, EH), CS ** -0.5, 0.375),
        "edge_in_weight": normal_values(splits[23], (CZ, EH), CZ ** -0.5, 0.5),
        "edge_out_weight": normal_values(splits[24], (EH, CZ), EH ** -0.5, 0.375),
    }


linear_scale = math.sqrt(1.0 / 3.0)
masked_score = -1000000000.0
norm_epsilon = 1e-05

def exact_dot(left, right):
    return jnp.dot(left.astype(jnp.float32), right.astype(jnp.float32), precision=lax.Precision.HIGHEST)

def rotations(angles):
    cos_yaw = jnp.cos(angles[0])
    sin_yaw = jnp.sin(angles[0])
    cos_pitch = jnp.cos(angles[1])
    sin_pitch = jnp.sin(angles[1])
    cos_roll = jnp.cos(angles[2])
    sin_roll = jnp.sin(angles[2])
    first_row = jnp.stack([cos_yaw * cos_pitch, cos_yaw * sin_pitch * sin_roll - sin_yaw * cos_roll, cos_yaw * sin_pitch * cos_roll + sin_yaw * sin_roll], 0)
    second_row = jnp.stack([sin_yaw * cos_pitch, sin_yaw * sin_pitch * sin_roll + cos_yaw * cos_roll, sin_yaw * sin_pitch * cos_roll - cos_yaw * sin_roll], 0)
    third_row = jnp.stack([-sin_pitch, cos_pitch * sin_roll, cos_pitch * cos_roll], 0)
    return jnp.stack([first_row, second_row, third_row], 0)

def layer_norm(values, gain):
    centred = values - lax.optimization_barrier(jnp.mean(values, axis=-1, keepdims=True))
    variance = lax.optimization_barrier(jnp.mean(centred * centred, axis=-1, keepdims=True))
    return centred * lax.rsqrt(variance + norm_epsilon) * gain

def rounded_copy(values):
    return lax.optimization_barrier(values.astype(jnp.bfloat16)).astype(jnp.float32)

def finish_nodes(attended, node_rows, angle_rows, trans_rows, out_weight, first_gain, second_gain, gate_weight, up_weight, down_weight):
    row_count, heads = (attended.shape[0], attended.shape[1])
    global_points = attended[:, :, CH:CH + 3 * PV].reshape(row_count, heads, 3, PV) - trans_rows.T[:, None, :, None]
    local_points = jnp.einsum('bai,ihbp->ihap', rotations(angle_rows), global_points, precision=lax.Precision.HIGHEST)
    point_norms = jnp.sqrt(1.0 + lax.optimization_barrier(jnp.sum(local_points * local_points, axis=2)))
    features = jnp.concatenate([attended[:, :, :CH], local_points.reshape(row_count, heads, 3 * PV), point_norms, attended[:, :, CH + 3 * PV:]], axis=2)
    features = features.reshape(row_count, heads * features.shape[2]).astype(jnp.bfloat16)
    projected = exact_dot(features, out_weight)
    first_nodes = layer_norm(node_rows.astype(jnp.float32) + projected, first_gain)
    first_rounded = first_nodes.astype(jnp.bfloat16)
    gate = exact_dot(first_rounded, gate_weight)
    upward = exact_dot(first_rounded, up_weight)
    hidden = (jax.nn.silu(gate) * upward).astype(jnp.bfloat16)
    mixed = exact_dot(hidden, down_weight)
    return layer_norm(first_nodes + mixed, second_gain).astype(jnp.bfloat16)

def reference(node_query, query_angles, query_trans, query_chain, node_key, key_angles, key_trans, key_chain, pair_features, pair_mask, query_weight, key_weight, bias_weight, point_gain, chain_gain, out_weight, first_gain, second_gain, gate_weight, up_weight, down_weight, edge_query_weight, edge_key_weight, edge_in_weight, edge_out_weight):
    highest = lax.Precision.HIGHEST
    query_count = node_query.shape[0]
    key_count = node_key.shape[0]
    query_proj = exact_dot(node_query, query_weight).reshape(query_count, H, CH + 3 * PQ)
    query_vectors = rounded_copy(query_proj[:, :, :CH])
    query_points = jnp.einsum('abi,ihbp->ihap', rotations(query_angles), query_proj[:, :, CH:].reshape(query_count, H, 3, PQ), precision=highest) + query_trans.T[:, None, :, None]
    query_points = query_points.reshape(query_count, H, 3 * PQ)
    key_proj = exact_dot(node_key, key_weight).reshape(key_count, H, 2 * CH + 3 * PQ + 3 * PV)
    key_vectors = rounded_copy(key_proj[:, :, :CH])
    value_vectors = rounded_copy(key_proj[:, :, CH:2 * CH])
    key_frames = rotations(key_angles)
    key_points = jnp.einsum('abi,ihbp->ihap', key_frames, key_proj[:, :, 2 * CH:2 * CH + 3 * PQ].reshape(key_count, H, 3, PQ), precision=highest) + key_trans.T[:, None, :, None]
    key_points = key_points.reshape(key_count, H, 3 * PQ)
    value_points = jnp.einsum('abi,ihbp->ihap', key_frames, key_proj[:, :, 2 * CH + 3 * PQ:].reshape(key_count, H, 3, PV), precision=highest) + key_trans.T[:, None, :, None]
    value_points = value_points.reshape(key_count, H, 3 * PV)
    query_squares = lax.optimization_barrier(jnp.sum(query_points * query_points, axis=2)).T
    key_squares = lax.optimization_barrier(jnp.sum(key_points * key_points, axis=2)).T
    point_scale = point_gain * (math.sqrt(2.0 / (9.0 * PQ)) / 2.0)
    edge_keys = exact_dot(node_key, edge_key_weight)
    bias_float = bias_weight.astype(jnp.float32)
    edge_in_float = edge_in_weight.astype(jnp.float32)
    edge_out_float = edge_out_weight.astype(jnp.float32)
    block = math.gcd(query_count, 16)

    def one_block(index):
        begin = (index * block).astype(jnp.int32)

        def rows_of(values, axis):
            return lax.dynamic_slice_in_dim(values, begin, block, axis)
        tile = rows_of(pair_features, 1).astype(jnp.float32)
        bias = jnp.einsum('cij,ch->hij', tile, bias_float, precision=highest)
        inner = jnp.einsum('ihc,jhc->hij', rows_of(query_vectors, 0), key_vectors, precision=highest) / math.sqrt(CH)
        cross = jnp.einsum('ihd,jhd->hij', rows_of(query_points, 0), key_points, precision=highest)
        distance = rows_of(query_squares, 1)[:, :, None] + key_squares[:, None, :] - 2.0 * cross
        same_chain = (rows_of(query_chain, 0)[:, None] == key_chain[None, :]).astype(jnp.float32)
        scores = linear_scale * (inner + bias + chain_gain[:, None, None] * same_chain[None] - point_scale[:, None, None] * distance)
        scores = jnp.where(rows_of(pair_mask, 0)[None] == 1, scores, masked_score)
        row_max = lax.optimization_barrier(jnp.max(scores, axis=2))
        weights = jnp.exp(scores - row_max[:, :, None])
        totals = lax.optimization_barrier(jnp.sum(weights, axis=2))
        rounded_weights = rounded_copy(weights)
        vector_part = jnp.einsum('hij,jhc->ihc', rounded_weights, value_vectors, precision=highest)
        point_part = jnp.einsum('hij,jhd->ihd', weights, value_points, precision=highest)
        pair_part = jnp.einsum('hij,cij->ihc', rounded_weights, tile, precision=highest)
        attended = jnp.concatenate([vector_part, point_part, pair_part], axis=2) / totals.T[:, :, None]
        new_nodes = finish_nodes(attended, rows_of(node_query, 0), rows_of(query_angles, 1), rows_of(query_trans, 1), out_weight, first_gain, second_gain, gate_weight, up_weight, down_weight)
        edge_queries = exact_dot(new_nodes, edge_query_weight)
        edge_pre = jnp.einsum('cij,ce->eij', tile, edge_in_float, precision=highest) + edge_queries.T[:, :, None] + edge_keys.T[:, None, :]
        edge_hidden = rounded_copy(jnp.maximum(edge_pre, 0.0))
        edge_out = jnp.einsum('eij,ec->cij', edge_hidden, edge_out_float, precision=highest)
        return (new_nodes, (tile + edge_out).astype(jnp.bfloat16))
    nodes, pairs = lax.map(one_block, jnp.arange(query_count // block, dtype=jnp.int32))
    updated_nodes = nodes.reshape(query_count, CS)
    updated_pairs = jnp.moveaxis(pairs, 0, 1).reshape(CZ, query_count, key_count)
    return (updated_nodes, updated_pairs)
```

```python
import functools
import math

import jax
import jax.numpy as jnp
from jax import lax
from jax.experimental import pallas as pl
from jax.experimental.pallas import tpu as pltpu
from jax.sharding import PartitionSpec as P

CH = 16
PQ = 4
PV = 8
QCOLS = CH + 3 * PQ
KCOLS = 2 * CH + 3 * PQ + 3 * PV
FEATURES = CH + 4 * PV
SLOT = 64
ROWS = 16

linear_scale = math.sqrt(1.0 / 3.0)
masked_score = -1000000000.0
norm_epsilon = 1e-05
point_factor = math.sqrt(2.0 / (9.0 * PQ)) / 2.0

f32 = jnp.float32
bf16 = jnp.bfloat16


def params(mib):
    return pltpu.CompilerParams(vmem_limit_bytes=mib * 2**20)


def dot(left, right):
    return jnp.dot(left, right, preferred_element_type=f32)


def dot_nt(left, right):
    return lax.dot_general(left, right, (((1,), (1,)), ((), ())), preferred_element_type=f32)


def dot_tn(left, right):
    return lax.dot_general(left, right, (((0,), (0,)), ((), ())), preferred_element_type=f32)


def dot_tt(left, right):
    return lax.dot_general(left, right, (((0,), (1,)), ((), ())), preferred_element_type=f32)


def iota(shape, axis):
    return lax.broadcasted_iota(jnp.int32, shape, axis)


def rounded(values):
    return values.astype(bf16).astype(f32)


def rotation_rows(angles):
    cos, sin = jnp.cos(angles), jnp.sin(angles)
    cy, cp, cr = cos[0:1], cos[1:2], cos[2:3]
    sy, sp, sr = sin[0:1], sin[1:2], sin[2:3]
    return [
        [cy * cp, cy * sp * sr - sy * cr, cy * sp * cr + sy * sr],
        [sy * cp, sy * sp * sr + cy * cr, sy * sp * cr - cy * sr],
        [-sp, cp * sr, cp * cr],
    ]


def whole(array):
    return pl.BlockSpec(array.shape, lambda *_: (0,) * array.ndim)


SMEM = pl.BlockSpec(memory_space=pltpu.SMEM)


def project_kernel(
    blocks,
    place,
    point_own,
    point_other,
    chain_own,
    chain_other,
    query_nodes,
    query_angles,
    query_trans,
    query_chain,
    key_angles,
    key_trans,
    key_chain,
    query_weight_own,
    query_weight_other,
    key_weight_own,
    key_weight_other,
    bias_own,
    bias_other,
    edge_key_weight,
    *rest,
):
    key_blocks = rest[:blocks]
    scores, values, bias_spread, query_frames, edge_keys = rest[blocks : blocks + 5]
    keys, key_proj, query_proj, key_side, query_side, query_rows = rest[blocks + 5 :]
    sub, mine = place[0], place[1]
    local_heads = query_weight_own.shape[1] // QCOLS
    query_count, key_count = query_nodes.shape[0], keys.shape[0]
    half = scores.shape[1]
    share = key_blocks[0].shape[0]
    for step in range(blocks):
        source = lax.rem(mine - step + blocks, blocks)
        keys[pl.ds(pl.multiple_of(source * share, share), share), :] = key_blocks[step][...]
    nodes = keys[...]
    key_proj[0] = dot_tt(key_weight_own[...], nodes)
    key_proj[1] = dot_tt(key_weight_other[...], nodes)
    query_proj[0] = dot_tt(query_weight_own[...], query_nodes[...])
    query_proj[1] = dot_tt(query_weight_other[...], query_nodes[...])
    edge_keys[...] = dot_tt(edge_key_weight[...], nodes)

    channels = bias_own.shape[0] // 2
    spread = channels * ROWS
    for at, offset in enumerate((sub * channels, (1 - sub) * channels)):
        select = (iota((2 * channels, spread), 0) == offset + iota((2 * channels, spread), 1) // ROWS)
        select = select.astype(f32).astype(bf16)
        diagonal = iota((1, ROWS, spread), 1) == iota((1, ROWS, spread), 2) % ROWS
        for which, weight in enumerate((bias_own, bias_other)):
            row = dot_tn(weight[...], select)
            block = jnp.where(diagonal, row[:, None, :], 0.0).reshape(local_heads * ROWS, spread)
            begin = which * local_heads * ROWS
            bias_spread[begin : begin + local_heads * ROWS, at * spread : (at + 1) * spread] = block.astype(bf16)

    key_frames = rotation_rows(key_angles[...])
    query_rotation = rotation_rows(query_angles[...])
    frame_rows = [query_rotation[a][b] for a in range(3) for b in range(3)]
    frame_rows += [query_trans[a : a + 1, :] for a in range(3)]
    frame_rows += [query_chain[...].astype(f32)] + [jnp.zeros((1, query_count), f32)] * 3
    query_frames[...] = jnp.concatenate(frame_rows, axis=0).T
    centre = jnp.mean(query_trans[...], axis=1, keepdims=True)

    key_side[...] = jnp.zeros_like(key_side)
    query_side[...] = jnp.zeros_like(query_side)
    key_squares = []
    for head in range(2 * local_heads):
        which, at = divmod(head, local_heads)
        scale = (point_own if which == 0 else point_other)[at] * point_factor
        begin = at * KCOLS
        key_side[head, 0:CH] = rounded(key_proj[which, begin : begin + CH])
        values[head, 0:CH] = key_proj[which, begin + CH : begin + 2 * CH].astype(bf16)
        begin += 2 * CH
        local = [key_proj[which, begin + PQ * b : begin + PQ * (b + 1)] for b in range(3)]
        squares = jnp.zeros((1, key_count), f32)
        for a in range(3):
            moved = sum(key_frames[a][b] * local[b] for b in range(3)) + (
                key_trans[a : a + 1, :] - centre[a : a + 1]
            )
            squares = squares + jnp.sum(moved * moved, axis=0, keepdims=True)
            high = rounded(moved)
            key_side[head, CH + PQ * a : CH + PQ * (a + 1)] = high
            key_side[head, CH + PQ * (3 + a) : CH + PQ * (4 + a)] = moved - high
            key_side[head, CH + PQ * (6 + a) : CH + PQ * (7 + a)] = high
        key_squares.append(squares)
        begin += 3 * PQ
        local = [key_proj[which, begin + PV * b : begin + PV * (b + 1)] for b in range(3)]
        highs, lows = [], []
        for a in range(3):
            moved = sum(key_frames[a][b] * local[b] for b in range(3)) + key_trans[a : a + 1, :]
            highs.append(rounded(moved))
            lows.append(moved - highs[-1])
        values[head, CH : CH + 3 * PV] = jnp.concatenate(highs, axis=0).astype(bf16)
        values[head, CH + 3 * PV : CH + 6 * PV] = jnp.concatenate(lows, axis=0).astype(bf16)
        begin = at * QCOLS
        query_side[head, 0:CH] = rounded(query_proj[which, begin : begin + CH]) * (1.0 / math.sqrt(CH))
        begin += CH
        local = [query_proj[which, begin + PQ * b : begin + PQ * (b + 1)] for b in range(3)]
        squares = jnp.zeros((1, query_count), f32)
        for a in range(3):
            moved = sum(query_rotation[a][b] * local[b] for b in range(3)) + (
                query_trans[a : a + 1, :] - centre[a : a + 1]
            )
            squares = squares + jnp.sum(moved * moved, axis=0, keepdims=True)
            moved = moved * (2.0 * scale)
            high = rounded(moved)
            query_side[head, CH + PQ * a : CH + PQ * (a + 1)] = high
            query_side[head, CH + PQ * (3 + a) : CH + PQ * (4 + a)] = high
            query_side[head, CH + PQ * (6 + a) : CH + PQ * (7 + a)] = moved - high
        query_side[head, SLOT - 1 : SLOT] = squares * (-scale)
    for head in range(2 * local_heads):
        query_rows[head] = query_side[head].T
    begin = pl.multiple_of(sub * half, half)
    chains = query_frames[pl.ds(begin, half), 12:13]
    same = (chains == key_chain[...].astype(f32)).astype(f32)
    for head in range(2 * local_heads):
        which, at = divmod(head, local_heads)
        scale = (point_own if which == 0 else point_other)[at] * point_factor
        chain_gain = (chain_own if which == 0 else chain_other)[at]
        left = query_rows[head, pl.ds(begin, half), :]
        score = dot(left.astype(bf16), key_side[head].astype(bf16))
        score = score + left[:, SLOT - 1 : SLOT] - scale * key_squares[head] + chain_gain * same
        scores[head] = linear_scale * score


def project(
    place, gains, query_side, key_side, query_weights, key_weights, bias_weights, edge_key_weight, key_blocks, half
):
    query_count = query_side[0].shape[0]
    key_count = key_side[0].shape[1]
    local_heads = gains[0].shape[0]
    heads = 2 * local_heads
    channels, hidden = bias_weights[0].shape[0], edge_key_weight.shape[1]
    operands = [*query_side, *key_side, *query_weights, *key_weights, *bias_weights, edge_key_weight, *key_blocks]
    return pl.pallas_call(
        functools.partial(project_kernel, len(key_blocks)),
        in_specs=[SMEM] * 5 + [whole(a) for a in operands],
        out_shape=(
            jax.ShapeDtypeStruct((heads, half, key_count), f32),
            jax.ShapeDtypeStruct((heads, SLOT, key_count), bf16),
            jax.ShapeDtypeStruct((heads * ROWS, channels * ROWS), bf16),
            jax.ShapeDtypeStruct((query_count, 16), f32),
            jax.ShapeDtypeStruct((hidden, key_count), f32),
        ),
        scratch_shapes=[
            pltpu.VMEM((key_count, query_side[0].shape[1]), bf16),
            pltpu.VMEM((2, local_heads * KCOLS, key_count), f32),
            pltpu.VMEM((2, local_heads * QCOLS, query_count), f32),
            pltpu.VMEM((heads, SLOT, key_count), f32),
            pltpu.VMEM((heads, SLOT, query_count), f32),
            pltpu.VMEM((heads, query_count, SLOT), f32),
        ],
        compiler_params=params(32),
        name="project",
    )(place, *gains, *operands)


def attend_kernel(
    place,
    own_pairs,
    other_pairs,
    base_scores,
    mask,
    values,
    bias_spread,
    frames,
    part,
    weight_high,
    weight_low,
    peaks,
    sums,
    gather_own,
    gather_other,
):
    step = pl.program_id(0)
    sub = place[0]
    heads, _, keys = base_scores.shape
    channels = own_pairs.shape[0]
    spread = channels * ROWS
    lanes = 2 * channels

    @pl.when(step == 0)
    def _():
        source = iota((spread, lanes), 0) // ROWS
        target = iota((spread, lanes), 1)
        gather_own[...] = (target == source + sub * channels).astype(f32).astype(bf16)
        gather_other[...] = (target == source + (1 - sub) * channels).astype(f32).astype(bf16)

    own = own_pairs[...].reshape(spread, keys)
    other = other_pairs[...].reshape(spread, keys)
    bias = dot(bias_spread[:, :spread], own) + dot(bias_spread[:, spread:], other)
    score = base_scores[...] + linear_scale * bias.reshape(heads, ROWS, keys)
    score = jnp.where(mask[...][None] == 1, score, masked_score)
    peak = jnp.max(score, axis=2, keepdims=True)
    weight = jnp.exp(score - peak)
    total = jnp.sum(weight, axis=2, keepdims=True)
    high = weight.astype(bf16)
    begin = pl.multiple_of(step * ROWS, ROWS)
    weight_high[:, pl.ds(begin, ROWS), :] = high
    weight_low[:, pl.ds(begin, ROWS), :] = (weight - high.astype(f32)).astype(bf16)
    peaks[:, pl.ds(begin, ROWS), :] = jnp.broadcast_to(peak, (heads, ROWS, lanes))
    sums[:, pl.ds(begin, ROWS), :] = jnp.broadcast_to(total, (heads, ROWS, lanes))
    flat = high.reshape(heads * ROWS, keys)
    scale = (1.0 / total).reshape(heads * ROWS, 1)
    diagonal = iota((heads * ROWS, spread), 0) % ROWS == iota((heads * ROWS, spread), 1) % ROWS
    own_part = jnp.where(diagonal, dot_nt(flat, own) * scale, 0.0).astype(bf16)
    other_part = jnp.where(diagonal, dot_nt(flat, other) * scale, 0.0).astype(bf16)
    pairs = dot(own_part, gather_own[...]) + dot(other_part, gather_other[...])
    part[0:heads, pl.ds(begin, ROWS), :] = pairs.reshape(heads, ROWS, lanes).astype(bf16)

    @pl.when(step == pl.num_programs(0) - 1)
    def _():
        half = frames.shape[0]
        lane = iota((half, 2 * SLOT), 1)
        first = lane < SLOT
        slot = lane % SLOT
        plane = (slot - CH) // PV
        inside = (slot >= CH) & (slot < CH + 3 * PV)

        def on_planes(columns):
            out = jnp.zeros((half, 2 * SLOT), f32)
            for b, column in columns:
                out = jnp.where(inside & (plane == b), frames[:, column : column + 1], out)
            return out

        shift = on_planes([(a, 9 + a) for a in range(3)])
        turns = [
            (d, on_planes([(b, 3 * (b - d) + b) for b in range(3) if 0 <= b - d < 3])) for d in range(-2, 3)
        ]
        for pair in range(heads // 2):
            a, b = 2 * pair, 2 * pair + 1
            left = jnp.concatenate([weight_high[a], weight_low[a], weight_high[b], weight_low[b]], axis=0)
            right = jnp.concatenate([values[a], values[b]], axis=0)
            out = dot_nt(left, right)
            upper = jnp.where(first, out[0:half], out[2 * half : 3 * half])
            lower = jnp.where(first, out[half : 2 * half], out[3 * half :])
            peak_pair = jnp.where(first, peaks[a], peaks[b])
            sum_pair = jnp.where(first, sums[a], sums[b])
            inverse = 1.0 / sum_pair
            points = (upper + lower + pltpu.roll(upper, 2 * SLOT - 3 * PV, 1)) * inverse - shift
            turned = jnp.zeros((half, 2 * SLOT), f32)
            for d, factor in turns:
                turned = turned + factor * (pltpu.roll(points, (d * PV) % (2 * SLOT), 1) if d else points)
            result = jnp.where(slot < CH, upper * inverse, turned)
            at = CH + 3 * PV
            for value in (peak_pair, sum_pair):
                for _ in range(3):
                    piece = rounded(value)
                    result = jnp.where(slot == at, piece, result)
                    value = value - piece
                    at += 1
            part[heads + pair] = jnp.where(slot < at, result, 0.0).astype(bf16)


def attend(place, own_pairs, other_pairs, base_scores, mask, values, bias_spread, frames):
    heads, half, keys = base_scores.shape
    channels = own_pairs.shape[0]
    steps = half // ROWS
    pair_block = pl.BlockSpec((channels, ROWS, keys), lambda g, p: (0, p[0] * steps + g, 0))
    return pl.pallas_call(
        attend_kernel,
        grid_spec=pltpu.PrefetchScalarGridSpec(
            num_scalar_prefetch=1,
            grid=(steps,),
            in_specs=[
                pair_block,
                pair_block,
                pl.BlockSpec((heads, ROWS, keys), lambda g, p: (0, g, 0)),
                pl.BlockSpec((ROWS, keys), lambda g, p: (p[0] * steps + g, 0)),
                whole(values),
                whole(bias_spread),
                pl.BlockSpec((half, frames.shape[1]), lambda g, p: (p[0], 0)),
            ],
            out_specs=pl.BlockSpec((heads + heads // 2, half, 2 * channels), lambda g, p: (0, 0, 0)),
            scratch_shapes=[
                pltpu.VMEM((heads, half, keys), bf16),
                pltpu.VMEM((heads, half, keys), bf16),
                pltpu.VMEM((heads, half, 2 * channels), f32),
                pltpu.VMEM((heads, half, 2 * channels), f32),
                pltpu.VMEM((channels * ROWS, 2 * channels), bf16),
                pltpu.VMEM((channels * ROWS, 2 * channels), bf16),
            ],
        ),
        out_shape=jax.ShapeDtypeStruct((heads + heads // 2, half, 2 * channels), bf16),
        compiler_params=params(40),
        name="attend",
    )(place, own_pairs, other_pairs, base_scores, mask, values, bias_spread, frames)


def norm(values, gain):
    centred = values - jnp.mean(values, axis=-1, keepdims=True)
    variance = jnp.mean(centred * centred, axis=-1, keepdims=True)
    return centred * lax.rsqrt(variance + norm_epsilon) * gain


def node_kernel(
    count,
    nodes,
    out_own,
    out_other,
    first_gain,
    second_gain,
    gate_weight,
    up_weight,
    down_weight,
    *rest,
):
    parts, result = rest[:count], rest[count]
    heads = parts[0].shape[0] * 2 // 3
    rows, lanes = parts[0].shape[1:]
    local_heads = heads // 2
    tall = local_heads * rows
    first = iota((tall, lanes), 1) < SLOT
    slot = iota((tall, lanes), 1) % SLOT
    at = CH + 3 * PV

    def broadcast(values, lane):
        return jnp.where(
            first,
            jnp.broadcast_to(values[:, lane : lane + 1], (tall, lanes)),
            jnp.broadcast_to(values[:, SLOT + lane : SLOT + lane + 1], (tall, lanes)),
        )

    extras, peaks, sums = [], [], []
    for part in parts:
        extra = part[heads:].astype(f32).reshape(tall, lanes)
        joined = extra + pltpu.roll(extra, lanes - 1, 1) + pltpu.roll(extra, lanes - 2, 1)
        extras.append(extra)
        peaks.append(broadcast(joined, at))
        sums.append(broadcast(joined, at + 3))
    peak = functools.reduce(jnp.maximum, peaks)
    shares = [s * jnp.exp(p - peak) for s, p in zip(sums, peaks)]
    total = sum(shares)
    shares = [s / total for s in shares]
    merged = sum(s * e for s, e in zip(shares, extras))
    squares = merged * merged
    norms = jnp.sqrt(
        1.0 + pltpu.roll(squares, PV, 1) + pltpu.roll(squares, 2 * PV, 1) + pltpu.roll(squares, 3 * PV, 1)
    )
    merged = jnp.where(slot < at, merged, norms).astype(bf16)
    projected = jnp.zeros((rows, nodes.shape[1]), f32)
    for head in range(heads):
        pair, odd = divmod(head, 2)
        weight = out_own if head < local_heads else out_other
        begin = (head % local_heads) * (FEATURES + lanes)
        span = slice(pair * rows, (pair + 1) * rows)
        lane = odd * SLOT
        mixed = jnp.zeros((rows, lanes), f32)
        for share, part in zip(shares, parts):
            factor = jnp.broadcast_to(share[span, lane : lane + 1], (rows, lanes))
            mixed = mixed + factor * part[head].astype(f32)
        projected = projected + dot(mixed.astype(bf16), weight[begin + FEATURES : begin + FEATURES + lanes])
        projected = projected + dot(merged[span, lane : lane + FEATURES], weight[begin : begin + FEATURES])
    first_nodes = norm(nodes[...].astype(f32) + projected, first_gain[...])
    first_rounded = first_nodes.astype(bf16)
    gate = dot(first_rounded, gate_weight[...])
    hidden = (gate / (1.0 + jnp.exp(-gate)) * dot(first_rounded, up_weight[...])).astype(bf16)
    result[...] = norm(first_nodes + dot(hidden, down_weight[...]), second_gain[...]).astype(bf16)


def update_nodes(parts, nodes, out_own, out_other, first_gain, second_gain, gate_weight, up_weight, down_weight):
    operands = [nodes, out_own, out_other, first_gain, second_gain, gate_weight, up_weight, down_weight, *parts]
    return pl.pallas_call(
        functools.partial(node_kernel, len(parts)),
        in_specs=[whole(a) for a in operands],
        out_shape=jax.ShapeDtypeStruct(nodes.shape, bf16),
        compiler_params=params(32),
        name="nodes",
    )(*operands)


def edge_kernel(
    place,
    own_pairs,
    other_pairs,
    nodes,
    edge_keys,
    in_weight,
    out_weight,
    query_weight,
    result,
    new_nodes,
    left,
    out_left,
    turned,
    hidden,
    fresh,
):
    channels, rows, keys = own_pairs.shape
    both = 2 * channels
    sub = place[0]

    @pl.when(pl.program_id(0) == 0)
    def _():
        own = pl.multiple_of(sub * channels, channels)
        other = pl.multiple_of((1 - sub) * channels, channels)
        left[:, 0:channels] = in_weight[pl.ds(own, channels), :].astype(f32).T.astype(bf16)
        left[:, channels:both] = in_weight[pl.ds(other, channels), :].astype(f32).T.astype(bf16)
        flipped = out_weight[...].astype(f32).T
        out_left[...] = jnp.where(sub == 0, flipped[0:channels], flipped[channels:]).astype(bf16)
        picks = iota((rows, 2 * rows, keys), 1) % rows == iota((rows, 2 * rows, keys), 0)
        turned[:, both:, :] = picks.astype(f32).astype(bf16)

    new_nodes[...] = nodes[0, 0]
    queries = dot_tt(query_weight[...], nodes[0, 0])
    high = queries.astype(bf16)
    left[:, both : both + rows] = high
    left[:, both + rows :] = (queries - high.astype(f32)).astype(bf16)
    turned[:, 0:channels, :] = jnp.swapaxes(own_pairs[...], 0, 1)
    turned[:, channels:both, :] = jnp.swapaxes(other_pairs[...], 0, 1)
    for row in range(rows):
        hidden[row] = jnp.maximum(dot(left[...], turned[row]) + edge_keys[...], 0.0).astype(bf16)
    for row in range(rows):
        out = dot(out_left[...], hidden[row])
        for at in range(keys // 128):
            fresh[at, pl.ds(row, channels, stride=rows), :] = out[:, at * 128 : (at + 1) * 128]
    for at in range(keys // 128):
        span = slice(at * 128, (at + 1) * 128)
        old = own_pairs[:, :, span].reshape(channels * rows, 128).astype(f32)
        result[:, :, span] = (old + fresh[at]).astype(bf16).reshape(channels, rows, 128)


def update_pairs(place, own_pairs, other_pairs, nodes, edge_keys, in_weight, out_weight, query_weight):
    channels, count, keys = own_pairs.shape
    hidden = in_weight.shape[1]
    features = nodes.shape[-1]
    steps = nodes.shape[1]
    pair_block = pl.BlockSpec((channels, ROWS, keys), lambda g, p: (0, g, 0))

    def node_block(g, p):
        return (lax.rem(g // steps + p[0], 2), lax.rem(lax.rem(g, steps) + p[1], steps), 0, 0)

    return pl.pallas_call(
        edge_kernel,
        grid_spec=pltpu.PrefetchScalarGridSpec(
            num_scalar_prefetch=1,
            grid=(count // ROWS,),
            in_specs=[
                pair_block,
                pair_block,
                pl.BlockSpec((1, 1, ROWS, features), node_block),
                whole(edge_keys),
                whole(in_weight),
                whole(out_weight),
                whole(query_weight),
            ],
            out_specs=(pair_block, pl.BlockSpec((ROWS, features), lambda g, p: (g, 0))),
            scratch_shapes=[
                pltpu.VMEM((hidden, 2 * channels + 2 * ROWS), bf16),
                pltpu.VMEM((channels, hidden), bf16),
                pltpu.VMEM((ROWS, 2 * channels + 2 * ROWS, keys), bf16),
                pltpu.VMEM((ROWS, hidden, keys), bf16),
                pltpu.VMEM((keys // 128, channels * ROWS, 128), f32),
            ],
        ),
        out_shape=(
            jax.ShapeDtypeStruct(own_pairs.shape, bf16),
            jax.ShapeDtypeStruct((count, features), bf16),
        ),
        compiler_params=params(40),
        name="edges",
    )(place, own_pairs, other_pairs, nodes, edge_keys, in_weight, out_weight, query_weight)


def shards(
    node_query,
    query_angles,
    query_trans,
    query_chain,
    node_key,
    key_angles,
    key_trans,
    key_chain,
    pair_features,
    pair_mask,
    query_weight,
    key_weight,
    bias_weight,
    point_gain,
    chain_gain,
    out_weight,
    first_gain,
    second_gain,
    gate_weight,
    up_weight,
    down_weight,
    edge_query_weight,
    edge_key_weight,
    edge_in_weight,
    edge_out_weight,
):
    subs, cols, rows = lax.axis_size("sub"), lax.axis_size("col"), lax.axis_size("row")
    sub, col = lax.axis_index("sub"), lax.axis_index("col")

    def swap(values):
        return lax.ppermute(values, "sub", [(i, (i + 1) % subs) for i in range(subs)])

    group = rows * subs
    mine = lax.axis_index(("row", "sub"))
    key_blocks = [node_key] + [
        lax.ppermute(node_key, ("row", "sub"), [(i, (i + k) % group) for i in range(group)])
        for k in range(1, group)
    ]
    other_query, other_key, other_bias = swap(query_weight), swap(key_weight), swap(bias_weight)
    other_point, other_chain = swap(point_gain), swap(chain_gain)
    other_pairs = swap(pair_features)
    other_out = swap(out_weight)

    query_count = node_query.shape[0]
    half = query_count // subs
    share = half // cols
    place = jnp.stack([sub, mine]).astype(jnp.int32)
    base_scores, values, bias_spread, frames, edge_keys = project(
        place,
        [point_gain, other_point, chain_gain, other_chain],
        [node_query, query_angles, query_trans, query_chain[None, :]],
        [key_angles, key_trans, key_chain[None, :]],
        [query_weight, other_query],
        [key_weight, other_key],
        [bias_weight, other_bias],
        edge_key_weight,
        key_blocks,
        half,
    )
    part = attend(place, pair_features, other_pairs, base_scores, pair_mask, values, bias_spread, frames)

    def piece(k):
        return lax.dynamic_slice_in_dim(part, lax.rem(col + k, cols) * share, share, 1)

    parts = [piece(0)] + [
        lax.ppermute(piece(k), "col", [(i, (i + k) % cols) for i in range(cols)]) for k in range(1, cols)
    ]
    spare = -share % ROWS
    own_nodes = lax.dynamic_slice_in_dim(node_query, sub * half + col * share, share, 0)
    if spare:
        parts = [jnp.pad(p, ((0, 0), (0, spare), (0, 0))) for p in parts]
        own_nodes = jnp.pad(own_nodes, ((0, spare), (0, 0)))
    fresh_nodes = update_nodes(
        parts,
        own_nodes,
        out_weight,
        other_out,
        first_gain[None, :],
        second_gain[None, :],
        gate_weight,
        up_weight,
        down_weight,
    )[:share]
    ring = [fresh_nodes] + [
        lax.ppermute(fresh_nodes, "col", [(i, (i - k) % cols) for i in range(cols)]) for k in range(1, cols)
    ]
    half_nodes = jnp.concatenate(ring, axis=0)
    if spare:
        half_nodes = jnp.roll(half_nodes, col * share, axis=0)
        turn = 0 * col
    else:
        turn = lax.rem(cols - col, cols) * (share // ROWS)
    both_nodes = jnp.stack([half_nodes, swap(half_nodes)])
    both_nodes = both_nodes.reshape(subs, half // ROWS, ROWS, node_query.shape[1])
    updated_pairs, updated_nodes = update_pairs(
        jnp.stack([sub, turn]).astype(jnp.int32),
        pair_features,
        other_pairs,
        both_nodes,
        edge_keys,
        edge_in_weight,
        edge_out_weight,
        edge_query_weight,
    )
    return (updated_nodes, updated_pairs)


def solution(mesh):
    return jax.shard_map(
        shards,
        mesh=mesh,
        in_specs=(
            P(("rep", "row"), None),
            P(None, ("rep", "row")),
            P(None, ("rep", "row")),
            P(("rep", "row")),
            P(("rep", "col", "row", "sub"), None),
            P(None, ("rep", "col")),
            P(None, ("rep", "col")),
            P(("rep", "col")),
            P("sub", ("rep", "row"), "col"),
            P(("rep", "row"), "col"),
            P(None, "sub"),
            P(None, "sub"),
            P(None, "sub"),
            P("sub"),
            P("sub"),
            P("sub", None),
            P(),
            P(),
            P(),
            P(),
            P(),
            P(),
            P(),
            P(),
            P(),
        ),
        out_specs=(P(("rep", "row"), None), P("sub", ("rep", "row"), "col")),
        check_vma=False,
    )
```

```python
import functools
import math

import jax
import jax.numpy as jnp
from jax import lax
from jax.experimental import pallas as pl
from jax.experimental.pallas import tpu as pltpu
from jax.sharding import PartitionSpec as P

CH = 16
PQ = 4
PV = 8
QCOLS = CH + 3 * PQ
KCOLS = 2 * CH + 3 * PQ + 3 * PV
FEATURES = CH + 4 * PV
SLOT = 64
ROWS = 16
VMEM_MIB = 60
CHUNKS = 4

linear_scale = math.sqrt(1.0 / 3.0)
masked_score = -1000000000.0
norm_epsilon = 1e-05
point_factor = math.sqrt(2.0 / (9.0 * PQ)) / 2.0

f32 = jnp.float32
bf16 = jnp.bfloat16


def params(mib):
    return pltpu.CompilerParams(vmem_limit_bytes=mib * 2**20)


def cost(microseconds):
    return pl.CostEstimate(flops=0, bytes_accessed=3_000_000 * microseconds, transcendentals=0)


def dot(left, right):
    return jnp.dot(left, right, preferred_element_type=f32)


def dot_nt(left, right):
    return lax.dot_general(left, right, (((1,), (1,)), ((), ())), preferred_element_type=f32)


def dot_tn(left, right):
    return lax.dot_general(left, right, (((0,), (0,)), ((), ())), preferred_element_type=f32)


def dot_tt(left, right):
    return lax.dot_general(left, right, (((0,), (1,)), ((), ())), preferred_element_type=f32)


def iota(shape, axis):
    return lax.broadcasted_iota(jnp.int32, shape, axis)


def rounded(values):
    return values.astype(bf16).astype(f32)


def rotation_rows(angles):
    cos, sin = jnp.cos(angles), jnp.sin(angles)
    cy, cp, cr = cos[0:1], cos[1:2], cos[2:3]
    sy, sp, sr = sin[0:1], sin[1:2], sin[2:3]
    return [
        [cy * cp, cy * sp * sr - sy * cr, cy * sp * cr + sy * sr],
        [sy * cp, sy * sp * sr + cy * cr, sy * sp * cr - cy * sr],
        [-sp, cp * sr, cp * cr],
    ]


def whole(array):
    return pl.BlockSpec(array.shape, lambda *_: (0,) * array.ndim)


SMEM = pl.BlockSpec(memory_space=pltpu.SMEM)


def up16(count):
    return -(-count // 16) * 16


def through(moves, buffer, arrivals, departures):
    starts, at = [], 0
    for step, (source, target) in enumerate(moves):
        end = at + source.shape[0]
        load = pltpu.make_async_copy(source, buffer.at[at:end], arrivals.at[step])
        load.start()
        starts.append((load, pltpu.make_async_copy(buffer.at[at:end], target, departures.at[step])))
        at = end
    return starts


def pass_on(starts):
    for load, store in starts:
        load.wait()
        store.start()
    for _, store in starts:
        store.wait()


def prepare_kernel(
    point_gain, chain_gain, key_weight, query_weight, bias_weight, pairs, packed, sliced, last, buffer, arrivals, departures
):
    half = sliced.shape[1]
    begin = pl.multiple_of((1 - lax.axis_index("sub")) * half, half)
    span = sliced.shape[0] // CHUNKS
    moves = [
        (pairs.at[at * span : (at + 1) * span, pl.ds(begin, half), :], sliced.at[at * span : (at + 1) * span])
        for at in range(CHUNKS)
    ]
    starts = through(moves, buffer, arrivals, departures)
    heads, channels = bias_weight.shape
    at = up16(key_weight.shape[0])
    end = at + up16(query_weight.shape[0])
    packed[0 : key_weight.shape[0]] = key_weight[...]
    packed[at : at + query_weight.shape[0]] = query_weight[...]
    row, lane = iota((16, 128), 0), iota((16, 128), 1)
    pieces = jnp.zeros((16, 128), f32)
    for which, gain in enumerate((point_gain, chain_gain)):
        value = jnp.zeros((16, 128), f32)
        for head in range(heads):
            value = jnp.where(row == head, gain[head], value)
        for step in range(3):
            piece = rounded(value)
            pieces = jnp.where(lane == 3 * which + step, piece, pieces)
            value = value - piece
    last[...] = jnp.zeros_like(last)
    last[0:heads, 0:channels] = bias_weight[...].astype(f32)
    last[:, channels : channels + 128] = pieces
    packed[end : end + 16] = last[...].astype(bf16)
    pass_on(starts)


def prepare(point_gain, chain_gain, key_weight, query_weight, bias_weight, pairs, half):
    operands = [key_weight, query_weight, bias_weight]
    total = up16(key_weight.shape[0]) + up16(query_weight.shape[0]) + 16
    hbm = pl.BlockSpec(memory_space=pl.ANY)
    shape = jax.ShapeDtypeStruct((total, key_weight.shape[1]), bf16)
    return pl.pallas_call(
        prepare_kernel,
        in_specs=[SMEM] * 2 + [whole(a) for a in operands] + [hbm],
        out_shape=(shape, jax.ShapeDtypeStruct((pairs.shape[0], half, pairs.shape[2]), bf16)),
        out_specs=(whole(shape), hbm),
        scratch_shapes=[
            pltpu.VMEM((16, key_weight.shape[1]), f32),
            pltpu.VMEM((pairs.shape[0], half, pairs.shape[2]), bf16),
            pltpu.SemaphoreType.DMA((CHUNKS,)),
            pltpu.SemaphoreType.DMA((CHUNKS,)),
        ],
        compiler_params=params(VMEM_MIB),
        cost_estimate=cost(2),
        name="prepare",
    )(point_gain, chain_gain, *operands, pairs)


def project_kernel(
    blocks,
    place,
    point_own,
    chain_own,
    query_nodes,
    query_angles,
    query_trans,
    query_chain,
    key_angles,
    key_trans,
    key_chain,
    query_weight_own,
    key_weight_own,
    bias_own,
    packed,
    edge_key_weight,
    *rest,
):
    key_blocks = rest[:blocks]
    scores, values, bias_spread, query_frames, edge_keys = rest[blocks : blocks + 5]
    keys, key_proj, query_proj, key_side, query_side, query_rows = rest[blocks + 5 :]
    sub, mine = place[0], place[1]
    local_heads = query_weight_own.shape[0] // QCOLS
    query_count, key_count = query_nodes.shape[0], keys.shape[0]
    half = scores.shape[1]
    share = key_blocks[0].shape[0]
    query_at = up16(local_heads * KCOLS)
    last_at = query_at + up16(local_heads * QCOLS)
    last = packed[last_at : last_at + 16].astype(f32)
    bias_other = last[0:local_heads, : bias_own.shape[1]].astype(bf16)
    gains = last[:, bias_own.shape[1] :]
    point_other = gains[:, 0:1] + gains[:, 1:2] + gains[:, 2:3]
    chain_other = gains[:, 3:4] + gains[:, 4:5] + gains[:, 5:6]
    for step in range(blocks):
        source = lax.rem(mine - step + blocks, blocks)
        keys[pl.ds(pl.multiple_of(source * share, share), share), :] = key_blocks[step][...]
    nodes = keys[...]
    key_proj[0] = dot_nt(key_weight_own[...], nodes)
    key_proj[1] = dot_nt(packed[: local_heads * KCOLS], nodes)
    query_proj[0] = dot_nt(query_weight_own[...], query_nodes[...])
    query_proj[1] = dot_nt(packed[query_at : query_at + local_heads * QCOLS], query_nodes[...])
    edge_keys[...] = dot_tt(edge_key_weight[...], nodes)

    channels = bias_own.shape[1] // 2
    spread = channels * ROWS
    for at, offset in enumerate((sub * channels, (1 - sub) * channels)):
        select = (iota((2 * channels, spread), 0) == offset + iota((2 * channels, spread), 1) // ROWS)
        select = select.astype(f32).astype(bf16)
        diagonal = iota((1, ROWS, spread), 1) == iota((1, ROWS, spread), 2) % ROWS
        for which, weight in enumerate((bias_own[...], bias_other)):
            row = dot(weight, select)
            block = jnp.where(diagonal, row[:, None, :], 0.0).reshape(local_heads * ROWS, spread)
            begin = which * local_heads * ROWS
            bias_spread[begin : begin + local_heads * ROWS, at * spread : (at + 1) * spread] = block.astype(bf16)

    key_frames = rotation_rows(key_angles[...])
    query_rotation = rotation_rows(query_angles[...])
    frame_rows = [query_rotation[a][b] for a in range(3) for b in range(3)]
    frame_rows += [query_trans[a : a + 1, :] for a in range(3)]
    frame_rows += [query_chain[...].astype(f32)] + [jnp.zeros((1, query_count), f32)] * 3
    query_frames[...] = jnp.concatenate(frame_rows, axis=0).T
    centre = jnp.mean(query_trans[...], axis=1, keepdims=True)

    key_side[...] = jnp.zeros_like(key_side)
    query_side[...] = jnp.zeros_like(query_side)
    key_squares = []
    for head in range(2 * local_heads):
        which, at = divmod(head, local_heads)
        scale = (point_own[at] if which == 0 else point_other[at : at + 1]) * point_factor
        begin = at * KCOLS
        key_side[head, 0:CH] = rounded(key_proj[which, begin : begin + CH])
        values[head, 0:CH] = key_proj[which, begin + CH : begin + 2 * CH].astype(bf16)
        begin += 2 * CH
        local = [key_proj[which, begin + PQ * b : begin + PQ * (b + 1)] for b in range(3)]
        squares = jnp.zeros((1, key_count), f32)
        for a in range(3):
            moved = sum(key_frames[a][b] * local[b] for b in range(3)) + (
                key_trans[a : a + 1, :] - centre[a : a + 1]
            )
            squares = squares + jnp.sum(moved * moved, axis=0, keepdims=True)
            high = rounded(moved)
            key_side[head, CH + PQ * a : CH + PQ * (a + 1)] = high
            key_side[head, CH + PQ * (3 + a) : CH + PQ * (4 + a)] = moved - high
            key_side[head, CH + PQ * (6 + a) : CH + PQ * (7 + a)] = high
        key_squares.append(squares)
        begin += 3 * PQ
        local = [key_proj[which, begin + PV * b : begin + PV * (b + 1)] for b in range(3)]
        highs, lows = [], []
        for a in range(3):
            moved = sum(key_frames[a][b] * local[b] for b in range(3)) + key_trans[a : a + 1, :]
            highs.append(rounded(moved))
            lows.append(moved - highs[-1])
        values[head, CH : CH + 3 * PV] = jnp.concatenate(highs, axis=0).astype(bf16)
        values[head, CH + 3 * PV : CH + 6 * PV] = jnp.concatenate(lows, axis=0).astype(bf16)
        begin = at * QCOLS
        query_side[head, 0:CH] = rounded(query_proj[which, begin : begin + CH]) * (1.0 / math.sqrt(CH))
        begin += CH
        local = [query_proj[which, begin + PQ * b : begin + PQ * (b + 1)] for b in range(3)]
        squares = jnp.zeros((1, query_count), f32)
        for a in range(3):
            moved = sum(query_rotation[a][b] * local[b] for b in range(3)) + (
                query_trans[a : a + 1, :] - centre[a : a + 1]
            )
            squares = squares + jnp.sum(moved * moved, axis=0, keepdims=True)
            moved = moved * (2.0 * scale)
            high = rounded(moved)
            query_side[head, CH + PQ * a : CH + PQ * (a + 1)] = high
            query_side[head, CH + PQ * (3 + a) : CH + PQ * (4 + a)] = high
            query_side[head, CH + PQ * (6 + a) : CH + PQ * (7 + a)] = moved - high
        query_side[head, SLOT - 1 : SLOT] = squares * (-scale)
    for head in range(2 * local_heads):
        query_rows[head] = query_side[head].T
    begin = pl.multiple_of(sub * half, half)
    chains = query_frames[pl.ds(begin, half), 12:13]
    same = (chains == key_chain[...].astype(f32)).astype(f32)
    for head in range(2 * local_heads):
        which, at = divmod(head, local_heads)
        scale = (point_own[at] if which == 0 else point_other[at : at + 1]) * point_factor
        chain_gain = chain_own[at] if which == 0 else chain_other[at : at + 1]
        left = query_rows[head, pl.ds(begin, half), :]
        score = dot(left.astype(bf16), key_side[head].astype(bf16))
        score = score + left[:, SLOT - 1 : SLOT] - scale * key_squares[head] + chain_gain * same
        scores[head] = linear_scale * score


def project(
    place, gains, query_side, key_side, query_weight, key_weight, bias_weight, packed, edge_key_weight, key_blocks, half
):
    query_count = query_side[0].shape[0]
    key_count = key_side[0].shape[1]
    local_heads = gains[0].shape[0]
    heads = 2 * local_heads
    channels, hidden = bias_weight.shape[1], edge_key_weight.shape[1]
    operands = [*query_side, *key_side, query_weight, key_weight, bias_weight, packed, edge_key_weight, *key_blocks]
    return pl.pallas_call(
        functools.partial(project_kernel, len(key_blocks)),
        in_specs=[SMEM] * 3 + [whole(a) for a in operands],
        out_shape=(
            jax.ShapeDtypeStruct((heads, half, key_count), f32),
            jax.ShapeDtypeStruct((heads, SLOT, key_count), bf16),
            jax.ShapeDtypeStruct((heads * ROWS, channels * ROWS), bf16),
            jax.ShapeDtypeStruct((query_count, 16), f32),
            jax.ShapeDtypeStruct((hidden, key_count), f32),
        ),
        scratch_shapes=[
            pltpu.VMEM((key_count, query_side[0].shape[1]), bf16),
            pltpu.VMEM((2, local_heads * KCOLS, key_count), f32),
            pltpu.VMEM((2, local_heads * QCOLS, query_count), f32),
            pltpu.VMEM((heads, SLOT, key_count), f32),
            pltpu.VMEM((heads, SLOT, query_count), f32),
            pltpu.VMEM((heads, query_count, SLOT), f32),
        ],
        compiler_params=params(VMEM_MIB),
        cost_estimate=cost(4),
        name="project",
    )(place, *gains, *operands)


def attend_kernel(
    place,
    own_pairs,
    other_pairs,
    base_scores,
    mask,
    values,
    bias_spread,
    frames,
    part,
    weight_high,
    weight_low,
    peaks,
    sums,
    gather_own,
    gather_other,
):
    step = pl.program_id(0)
    sub = place[0]
    heads, _, keys = base_scores.shape
    channels = own_pairs.shape[0]
    spread = channels * ROWS
    lanes = 2 * channels

    @pl.when(step == 0)
    def _():
        source = iota((spread, lanes), 0) // ROWS
        target = iota((spread, lanes), 1)
        gather_own[...] = (target == source + sub * channels).astype(f32).astype(bf16)
        gather_other[...] = (target == source + (1 - sub) * channels).astype(f32).astype(bf16)

    own = own_pairs[...].reshape(spread, keys)
    other = other_pairs[...].reshape(spread, keys)
    bias = dot(bias_spread[:, :spread], own) + dot(bias_spread[:, spread:], other)
    score = base_scores[...] + linear_scale * bias.reshape(heads, ROWS, keys)
    score = jnp.where(mask[...][None] == 1, score, masked_score)
    peak = jnp.max(score, axis=2, keepdims=True)
    weight = jnp.exp(score - peak)
    total = jnp.sum(weight, axis=2, keepdims=True)
    high = weight.astype(bf16)
    begin = pl.multiple_of(step * ROWS, ROWS)
    weight_high[:, pl.ds(begin, ROWS), :] = high
    weight_low[:, pl.ds(begin, ROWS), :] = (weight - high.astype(f32)).astype(bf16)
    peaks[:, pl.ds(begin, ROWS), :] = jnp.broadcast_to(peak, (heads, ROWS, lanes))
    sums[:, pl.ds(begin, ROWS), :] = jnp.broadcast_to(total, (heads, ROWS, lanes))
    flat = high.reshape(heads * ROWS, keys)
    scale = (1.0 / total).reshape(heads * ROWS, 1)
    diagonal = iota((heads * ROWS, spread), 0) % ROWS == iota((heads * ROWS, spread), 1) % ROWS
    own_part = jnp.where(diagonal, dot_nt(flat, own) * scale, 0.0).astype(bf16)
    other_part = jnp.where(diagonal, dot_nt(flat, other) * scale, 0.0).astype(bf16)
    pairs = dot(own_part, gather_own[...]) + dot(other_part, gather_other[...])
    part[0:heads, pl.ds(begin, ROWS), :] = pairs.reshape(heads, ROWS, lanes).astype(bf16)

    @pl.when(step == pl.num_programs(0) - 1)
    def _():
        half = frames.shape[0]
        lane = iota((half, 2 * SLOT), 1)
        first = lane < SLOT
        slot = lane % SLOT
        plane = (slot - CH) // PV
        inside = (slot >= CH) & (slot < CH + 3 * PV)

        def on_planes(columns):
            out = jnp.zeros((half, 2 * SLOT), f32)
            for b, column in columns:
                out = jnp.where(inside & (plane == b), frames[:, column : column + 1], out)
            return out

        shift = on_planes([(a, 9 + a) for a in range(3)])
        turns = [
            (d, on_planes([(b, 3 * (b - d) + b) for b in range(3) if 0 <= b - d < 3])) for d in range(-2, 3)
        ]
        for pair in range(heads // 2):
            a, b = 2 * pair, 2 * pair + 1
            left = jnp.concatenate([weight_high[a], weight_low[a], weight_high[b], weight_low[b]], axis=0)
            right = jnp.concatenate([values[a], values[b]], axis=0)
            out = dot_nt(left, right)
            upper = jnp.where(first, out[0:half], out[2 * half : 3 * half])
            lower = jnp.where(first, out[half : 2 * half], out[3 * half :])
            peak_pair = jnp.where(first, peaks[a], peaks[b])
            sum_pair = jnp.where(first, sums[a], sums[b])
            inverse = 1.0 / sum_pair
            points = (upper + lower + pltpu.roll(upper, 2 * SLOT - 3 * PV, 1)) * inverse - shift
            turned = jnp.zeros((half, 2 * SLOT), f32)
            for d, factor in turns:
                turned = turned + factor * (pltpu.roll(points, (d * PV) % (2 * SLOT), 1) if d else points)
            result = jnp.where(slot < CH, upper * inverse, turned)
            at = CH + 3 * PV
            for value in (peak_pair, sum_pair):
                for _ in range(3):
                    piece = rounded(value)
                    result = jnp.where(slot == at, piece, result)
                    value = value - piece
                    at += 1
            part[heads + pair] = jnp.where(slot < at, result, 0.0).astype(bf16)


def attend(place, own_pairs, other_pairs, base_scores, mask, values, bias_spread, frames):
    heads, half, keys = base_scores.shape
    channels = own_pairs.shape[0]
    steps = half // ROWS
    pair_block = pl.BlockSpec((channels, ROWS, keys), lambda g, p: (0, p[0] * steps + g, 0))
    return pl.pallas_call(
        attend_kernel,
        grid_spec=pltpu.PrefetchScalarGridSpec(
            num_scalar_prefetch=1,
            grid=(steps,),
            in_specs=[
                pair_block,
                pl.BlockSpec((channels, ROWS, keys), lambda g, p: (0, g, 0)),
                pl.BlockSpec((heads, ROWS, keys), lambda g, p: (0, g, 0)),
                pl.BlockSpec((ROWS, keys), lambda g, p: (p[0] * steps + g, 0)),
                whole(values),
                whole(bias_spread),
                pl.BlockSpec((half, frames.shape[1]), lambda g, p: (p[0], 0)),
            ],
            out_specs=pl.BlockSpec((heads + heads // 2, half, 2 * channels), lambda g, p: (0, 0, 0)),
            scratch_shapes=[
                pltpu.VMEM((heads, half, keys), bf16),
                pltpu.VMEM((heads, half, keys), bf16),
                pltpu.VMEM((heads, half, 2 * channels), f32),
                pltpu.VMEM((heads, half, 2 * channels), f32),
                pltpu.VMEM((channels * ROWS, 2 * channels), bf16),
                pltpu.VMEM((channels * ROWS, 2 * channels), bf16),
            ],
        ),
        out_shape=jax.ShapeDtypeStruct((heads + heads // 2, half, 2 * channels), bf16),
        compiler_params=params(VMEM_MIB),
        cost_estimate=cost(9),
        name="attend",
    )(place, own_pairs, other_pairs, base_scores, mask, values, bias_spread, frames)


def norm(values, gain):
    centred = values - jnp.mean(values, axis=-1, keepdims=True)
    variance = jnp.mean(centred * centred, axis=-1, keepdims=True)
    return centred * lax.rsqrt(variance + norm_epsilon) * gain


def node_kernel(
    count,
    nodes,
    out_own,
    out_other,
    first_gain,
    second_gain,
    gate_weight,
    up_weight,
    down_weight,
    *rest,
):
    parts, result = rest[:count], rest[count]
    heads = parts[0].shape[0] * 2 // 3
    rows, lanes = parts[0].shape[1:]
    local_heads = heads // 2
    tall = local_heads * rows
    first = iota((tall, lanes), 1) < SLOT
    slot = iota((tall, lanes), 1) % SLOT
    at = CH + 3 * PV

    def broadcast(values, lane):
        return jnp.where(
            first,
            jnp.broadcast_to(values[:, lane : lane + 1], (tall, lanes)),
            jnp.broadcast_to(values[:, SLOT + lane : SLOT + lane + 1], (tall, lanes)),
        )

    extras, peaks, sums = [], [], []
    for part in parts:
        extra = part[heads:].astype(f32).reshape(tall, lanes)
        joined = extra + pltpu.roll(extra, lanes - 1, 1) + pltpu.roll(extra, lanes - 2, 1)
        extras.append(extra)
        peaks.append(broadcast(joined, at))
        sums.append(broadcast(joined, at + 3))
    peak = functools.reduce(jnp.maximum, peaks)
    shares = [s * jnp.exp(p - peak) for s, p in zip(sums, peaks)]
    total = sum(shares)
    shares = [s / total for s in shares]
    merged = sum(s * e for s, e in zip(shares, extras))
    squares = merged * merged
    norms = jnp.sqrt(
        1.0 + pltpu.roll(squares, PV, 1) + pltpu.roll(squares, 2 * PV, 1) + pltpu.roll(squares, 3 * PV, 1)
    )
    merged = jnp.where(slot < at, merged, norms).astype(bf16)
    projected = jnp.zeros((rows, nodes.shape[1]), f32)
    for head in range(heads):
        pair, odd = divmod(head, 2)
        weight = out_own if head < local_heads else out_other
        begin = (head % local_heads) * (FEATURES + lanes)
        span = slice(pair * rows, (pair + 1) * rows)
        lane = odd * SLOT
        mixed = jnp.zeros((rows, lanes), f32)
        for share, part in zip(shares, parts):
            factor = jnp.broadcast_to(share[span, lane : lane + 1], (rows, lanes))
            mixed = mixed + factor * part[head].astype(f32)
        projected = projected + dot(mixed.astype(bf16), weight[begin + FEATURES : begin + FEATURES + lanes])
        projected = projected + dot(merged[span, lane : lane + FEATURES], weight[begin : begin + FEATURES])
    first_nodes = norm(nodes[...].astype(f32) + projected, first_gain[...])
    first_rounded = first_nodes.astype(bf16)
    gate = dot(first_rounded, gate_weight[...])
    hidden = (gate / (1.0 + jnp.exp(-gate)) * dot(first_rounded, up_weight[...])).astype(bf16)
    result[...] = norm(first_nodes + dot(hidden, down_weight[...]), second_gain[...]).astype(bf16)


def update_nodes(parts, nodes, out_own, out_other, first_gain, second_gain, gate_weight, up_weight, down_weight):
    operands = [nodes, out_own, out_other, first_gain, second_gain, gate_weight, up_weight, down_weight, *parts]
    return pl.pallas_call(
        functools.partial(node_kernel, len(parts)),
        in_specs=[whole(a) for a in operands],
        out_shape=jax.ShapeDtypeStruct(nodes.shape, bf16),
        compiler_params=params(16),
        cost_estimate=cost(2),
        name="nodes",
    )(*operands)


def turn_kernel(place, own_pairs, other_pairs, in_weight, out_weight, result, left, out_left):
    channels = own_pairs.shape[0]
    sub = place[0]

    @pl.when(pl.program_id(0) == 0)
    def _():
        own = pl.multiple_of(sub * channels, channels)
        other = pl.multiple_of((1 - sub) * channels, channels)
        left[:, 0:channels] = in_weight[pl.ds(own, channels), :].astype(f32).T.astype(bf16)
        left[:, channels:] = in_weight[pl.ds(other, channels), :].astype(f32).T.astype(bf16)
        flipped = out_weight[...].astype(f32).T
        out_left[0:channels] = jnp.where(sub == 0, flipped[0:channels], flipped[channels:]).astype(bf16)
        out_left[channels:] = jnp.where(sub == 0, flipped[channels:], flipped[0:channels]).astype(bf16)

    result[:, 0:channels, :] = jnp.swapaxes(own_pairs[...], 0, 1)
    result[:, channels:, :] = jnp.swapaxes(other_pairs[...], 0, 1)


def turn_pairs(place, own_pairs, other_pairs, in_weight, out_weight):
    channels, half, keys = other_pairs.shape
    both, hidden = in_weight.shape
    steps = half // ROWS
    return pl.pallas_call(
        turn_kernel,
        grid_spec=pltpu.PrefetchScalarGridSpec(
            num_scalar_prefetch=1,
            grid=(steps,),
            in_specs=[
                pl.BlockSpec((channels, ROWS, keys), lambda g, p: (0, p[0] * steps + g, 0)),
                pl.BlockSpec((channels, ROWS, keys), lambda g, p: (0, g, 0)),
                whole(in_weight),
                whole(out_weight),
            ],
            out_specs=(
                pl.BlockSpec((ROWS, both, keys), lambda g, p: (g, 0, 0)),
                pl.BlockSpec((hidden, both), lambda g, p: (0, 0)),
                pl.BlockSpec((both, hidden), lambda g, p: (0, 0)),
            ),
        ),
        out_shape=(
            jax.ShapeDtypeStruct((half, both, keys), bf16),
            jax.ShapeDtypeStruct((hidden, both), bf16),
            jax.ShapeDtypeStruct((both, hidden), bf16),
        ),
        compiler_params=params(VMEM_MIB),
        cost_estimate=cost(4),
        name="turn_pairs",
    )(place, own_pairs, other_pairs, in_weight, out_weight)


def edge_kernel(
    place, turned, nodes, edge_keys, in_left, out_left, query_weight, kept, sent, new_nodes, left, picks, hidden, fresh
):
    rows, both, keys = turned.shape
    channels = both // 2

    @pl.when(pl.program_id(0) == 0)
    def _():
        left[:, 0:both] = in_left[...]
        chosen = iota((rows, 2 * rows, keys), 1) % rows == iota((rows, 2 * rows, keys), 0)
        picks[...] = chosen.astype(f32).astype(bf16)

    queries = dot_tt(query_weight[...], nodes[0])
    high = queries.astype(bf16)
    left[:, both : both + rows] = high
    left[:, both + rows :] = (queries - high.astype(f32)).astype(bf16)
    new_nodes[...] = nodes[0]
    for at in range(sent.shape[0] - channels):
        sent[channels + at] = nodes[0, :, at * keys : (at + 1) * keys]
    for row in range(rows):
        right = jnp.concatenate([turned[row], picks[row]], axis=0)
        hidden[row] = jnp.maximum(dot(left[...], right) + edge_keys[...], 0.0).astype(bf16)
    for row in range(rows):
        old = turned[row].astype(f32)
        fresh[row] = (old + dot(out_left[...], hidden[row])).astype(bf16)
    kept[...] = jnp.swapaxes(fresh[:, 0:channels, :], 0, 1)
    sent[0:channels] = jnp.swapaxes(fresh[:, channels:, :], 0, 1)


def update_pairs(place, count, turned, nodes, edge_keys, in_left, out_left, query_weight):
    half, both, keys = turned.shape
    channels, hidden = both // 2, in_left.shape[0]
    steps, _, features = nodes.shape
    assert features % keys == 0
    extra = features // keys
    return pl.pallas_call(
        edge_kernel,
        grid_spec=pltpu.PrefetchScalarGridSpec(
            num_scalar_prefetch=1,
            grid=(steps,),
            in_specs=[
                pl.BlockSpec((ROWS, both, keys), lambda g, p: (g, 0, 0)),
                pl.BlockSpec((1, ROWS, features), lambda g, p: (lax.rem(g + p[1], steps), 0, 0)),
                whole(edge_keys),
                whole(in_left),
                whole(out_left),
                whole(query_weight),
            ],
            out_specs=(
                pl.BlockSpec((channels, ROWS, keys), lambda g, p: (0, p[0] * steps + g, 0)),
                pl.BlockSpec((channels + extra, ROWS, keys), lambda g, p: (0, g, 0)),
                pl.BlockSpec((ROWS, features), lambda g, p: (p[0] * steps + g, 0)),
            ),
            scratch_shapes=[
                pltpu.VMEM((hidden, both + 2 * ROWS), bf16),
                pltpu.VMEM((ROWS, 2 * ROWS, keys), bf16),
                pltpu.VMEM((ROWS, hidden, keys), bf16),
                pltpu.VMEM((ROWS, both, keys), bf16),
            ],
        ),
        out_shape=(
            jax.ShapeDtypeStruct((channels, count, keys), bf16),
            jax.ShapeDtypeStruct((channels + extra, half, keys), bf16),
            jax.ShapeDtypeStruct((count, features), bf16),
        ),
        compiler_params=params(VMEM_MIB),
        cost_estimate=cost(8),
        name="edges",
    )(place, turned, nodes, edge_keys, in_left, out_left, query_weight)


def finish_kernel(arrived, pairs_in, nodes_in, pairs, nodes, buffer, arrivals, departures):
    channels, half, keys = pairs.shape[0], arrived.shape[1], arrived.shape[2]
    begin = pl.multiple_of((1 - lax.axis_index("sub")) * half, half)
    rows = pl.ds(begin, half)
    span = channels // CHUNKS
    moves = [
        (arrived.at[at * span : (at + 1) * span], pairs.at[at * span : (at + 1) * span, rows, :])
        for at in range(CHUNKS)
    ]
    starts = through(moves, buffer, arrivals, departures)
    for at in range(arrived.shape[0] - channels):
        source = arrived.at[channels + at]
        load = pltpu.make_async_copy(source, buffer.at[channels + at], arrivals.at[CHUNKS + at])
        target = nodes.at[rows, at * keys : (at + 1) * keys]
        load.start()
        starts.append((load, pltpu.make_async_copy(buffer.at[channels + at], target, departures.at[CHUNKS + at])))
    pass_on(starts)


def finish(arrived, pairs, nodes):
    hbm = pl.BlockSpec(memory_space=pl.ANY)
    copies = CHUNKS + arrived.shape[0] - pairs.shape[0]
    return pl.pallas_call(
        finish_kernel,
        in_specs=[hbm] * 3,
        out_specs=(hbm, hbm),
        out_shape=(
            jax.ShapeDtypeStruct(pairs.shape, bf16),
            jax.ShapeDtypeStruct(nodes.shape, bf16),
        ),
        scratch_shapes=[
            pltpu.VMEM(arrived.shape, bf16),
            pltpu.SemaphoreType.DMA((copies,)),
            pltpu.SemaphoreType.DMA((copies,)),
        ],
        input_output_aliases={1: 0, 2: 1},
        compiler_params=params(62),
        cost_estimate=cost(1),
        name="finish",
    )(arrived, pairs, nodes)


def shards(
    node_query,
    query_angles,
    query_trans,
    query_chain,
    node_key,
    key_angles,
    key_trans,
    key_chain,
    pair_features,
    pair_mask,
    query_weight,
    key_weight,
    bias_weight,
    point_gain,
    chain_gain,
    out_weight,
    first_gain,
    second_gain,
    gate_weight,
    up_weight,
    down_weight,
    edge_query_weight,
    edge_key_weight,
    edge_in_weight,
    edge_out_weight,
):
    subs, cols, rows = lax.axis_size("sub"), lax.axis_size("col"), lax.axis_size("row")
    sub, col = lax.axis_index("sub"), lax.axis_index("col")

    def swap(values):
        return lax.ppermute(values, "sub", [(i, (i + 1) % subs) for i in range(subs)])

    group = rows * subs
    key_blocks = [node_key] + [
        lax.ppermute(node_key, ("row", "sub"), [(i, (i + k) % group) for i in range(group)])
        for k in range(1, group)
    ]
    half = node_query.shape[0] // subs
    query_weight, key_weight, bias_weight = query_weight.T, key_weight.T, bias_weight.T
    packed, late_pairs = prepare(
        point_gain, chain_gain, key_weight, query_weight, bias_weight, pair_features, half
    )
    packed = swap(packed)
    other_pairs = swap(late_pairs)

    share = half // cols
    place = jnp.stack([sub, lax.axis_index(("row", "sub"))]).astype(jnp.int32)
    base_scores, values, bias_spread, frames, edge_keys = project(
        place,
        [point_gain, chain_gain],
        [node_query, query_angles, query_trans, query_chain[None, :]],
        [key_angles, key_trans, key_chain[None, :]],
        query_weight,
        key_weight,
        bias_weight,
        packed,
        edge_key_weight,
        key_blocks,
        half,
    )
    part = attend(place, pair_features, other_pairs, base_scores, pair_mask, values, bias_spread, frames)
    other_out = swap(lax.optimization_barrier((out_weight, base_scores))[0])

    def piece(k):
        return lax.dynamic_slice_in_dim(part, lax.rem(col + k, cols) * share, share, 1)

    pieces = [piece(k) for k in range(cols)]
    parts = [pieces[0]] + [
        lax.ppermute(pieces[k], "col", [(i, (i + k) % cols) for i in range(cols)]) for k in range(1, cols)
    ]
    spare = -share % ROWS
    own_nodes = lax.dynamic_slice_in_dim(node_query, sub * half + col * share, share, 0)
    if spare:
        parts = [jnp.pad(p, ((0, 0), (0, spare), (0, 0))) for p in parts]
        own_nodes = jnp.pad(own_nodes, ((0, spare), (0, 0)))
    turn_place, _ = lax.optimization_barrier((place, pieces))
    turned, in_left, out_left = turn_pairs(
        turn_place, pair_features, other_pairs, edge_in_weight, edge_out_weight
    )
    own_nodes, turned = lax.optimization_barrier((own_nodes, turned))
    fresh_nodes = update_nodes(
        parts,
        own_nodes,
        out_weight,
        other_out,
        first_gain[None, :],
        second_gain[None, :],
        gate_weight,
        up_weight,
        down_weight,
    )[:share]
    ring = [fresh_nodes] + [
        lax.ppermute(fresh_nodes, "col", [(i, (i - k) % cols) for i in range(cols)]) for k in range(1, cols)
    ]
    near_nodes = jnp.concatenate(ring, axis=0)
    if spare:
        near_nodes = jnp.roll(near_nodes, col * share, axis=0)
        turn = 0 * col
    else:
        turn = lax.rem(cols - col, cols) * (share // ROWS)
    near_nodes = near_nodes.reshape(half // ROWS, ROWS, near_nodes.shape[1])
    edge_place = jnp.stack([sub, turn]).astype(jnp.int32)
    kept, sent, new_nodes = update_pairs(
        edge_place, pair_features.shape[1], turned, near_nodes, edge_keys, in_left, out_left, edge_query_weight
    )
    updated_pairs, updated_nodes = finish(swap(sent), kept, new_nodes)
    return (updated_nodes, updated_pairs)


def solution(mesh):
    return jax.shard_map(
        shards,
        mesh=mesh,
        in_specs=(
            P(("rep", "row"), None),
            P(None, ("rep", "row")),
            P(None, ("rep", "row")),
            P(("rep", "row")),
            P(("rep", "col", "row", "sub"), None),
            P(None, ("rep", "col")),
            P(None, ("rep", "col")),
            P(("rep", "col")),
            P("sub", ("rep", "row"), "col"),
            P(("rep", "row"), "col"),
            P(None, "sub"),
            P(None, "sub"),
            P(None, "sub"),
            P("sub"),
            P("sub"),
            P("sub", None),
            P(),
            P(),
            P(),
            P(),
            P(),
            P(),
            P(),
            P(),
            P(),
        ),
        out_specs=(P(("rep", "row"), None), P("sub", ("rep", "row"), "col")),
        check_vma=False,
    )
```

```python
import functools
import math

import jax
import jax.numpy as jnp
from jax import lax
from jax.experimental import pallas as pl
from jax.experimental.pallas import tpu as pltpu
from jax.sharding import PartitionSpec as P

CH = 16
PQ = 4
PV = 8
QCOLS = CH + 3 * PQ
KCOLS = 2 * CH + 3 * PQ + 3 * PV
FEATURES = CH + 4 * PV
SLOT = 64
ROWS = 16
VMEM_MIB = 60
CHUNKS = 4
ATTEND_ROWS = 32
TURN_ROWS = 32
EDGE_ROWS = 16

linear_scale = math.sqrt(1.0 / 3.0)
masked_score = -1000000000.0
norm_epsilon = 1e-05
point_factor = math.sqrt(2.0 / (9.0 * PQ)) / 2.0

f32 = jnp.float32
bf16 = jnp.bfloat16


def params(mib):
    return pltpu.CompilerParams(vmem_limit_bytes=mib * 2**20)


def cost(microseconds):
    return pl.CostEstimate(flops=0, bytes_accessed=3_000_000 * microseconds, transcendentals=0)


def dot(left, right):
    return jnp.dot(left, right, preferred_element_type=f32)


def dot_nt(left, right):
    return lax.dot_general(left, right, (((1,), (1,)), ((), ())), preferred_element_type=f32)


def dot_tn(left, right):
    return lax.dot_general(left, right, (((0,), (0,)), ((), ())), preferred_element_type=f32)


def dot_tt(left, right):
    return lax.dot_general(left, right, (((0,), (1,)), ((), ())), preferred_element_type=f32)


def iota(shape, axis):
    return lax.broadcasted_iota(jnp.int32, shape, axis)


def rounded(values):
    return values.astype(bf16).astype(f32)


def rotation_rows(angles):
    cos, sin = jnp.cos(angles), jnp.sin(angles)
    cy, cp, cr = cos[0:1], cos[1:2], cos[2:3]
    sy, sp, sr = sin[0:1], sin[1:2], sin[2:3]
    return [
        [cy * cp, cy * sp * sr - sy * cr, cy * sp * cr + sy * sr],
        [sy * cp, sy * sp * sr + cy * cr, sy * sp * cr - cy * sr],
        [-sp, cp * sr, cp * cr],
    ]


def whole(array):
    return pl.BlockSpec(array.shape, lambda *_: (0,) * array.ndim)


SMEM = pl.BlockSpec(memory_space=pltpu.SMEM)


def up16(count):
    return -(-count // 16) * 16


def pack_kernel(point_gain, chain_gain, key_weight, query_weight, bias_weight, nodes, packed, last):
    heads, channels = bias_weight.shape
    at = up16(key_weight.shape[0])
    end = at + up16(query_weight.shape[0])
    packed[0 : key_weight.shape[0]] = key_weight[...]
    packed[at : at + query_weight.shape[0]] = query_weight[...]
    row, lane = iota((16, 128), 0), iota((16, 128), 1)
    pieces = jnp.zeros((16, 128), f32)
    for which, gain in enumerate((point_gain, chain_gain)):
        value = jnp.zeros((16, 128), f32)
        for head in range(heads):
            value = jnp.where(row == head, gain[head], value)
        for step in range(3):
            piece = rounded(value)
            pieces = jnp.where(lane == 3 * which + step, piece, pieces)
            value = value - piece
    last[...] = jnp.zeros_like(last)
    last[0:heads, 0:channels] = bias_weight[...].astype(f32)
    last[:, channels : channels + 128] = pieces
    packed[end : end + 16] = last[...].astype(bf16)
    packed[end + 16 :] = nodes[...]


def pack(point_gain, chain_gain, key_weight, query_weight, bias_weight, nodes):
    operands = [key_weight, query_weight, bias_weight, nodes]
    total = up16(key_weight.shape[0]) + up16(query_weight.shape[0]) + 16 + nodes.shape[0]
    return pl.pallas_call(
        pack_kernel,
        in_specs=[SMEM] * 2 + [whole(a) for a in operands],
        out_shape=jax.ShapeDtypeStruct((total, key_weight.shape[1]), bf16),
        scratch_shapes=[pltpu.VMEM((16, key_weight.shape[1]), f32)],
        compiler_params=params(63),
        cost_estimate=cost(2),
        name="pack",
    )(point_gain, chain_gain, *operands)


def slice_kernel(pairs, sliced, buffer, arrivals, departures):
    half = sliced.shape[1]
    begin = pl.multiple_of((1 - lax.axis_index("sub")) * half, half)
    span = sliced.shape[0] // CHUNKS
    copies = []
    for chunk in range(CHUNKS):
        at = slice(chunk * span, (chunk + 1) * span)
        load = pltpu.make_async_copy(pairs.at[at, pl.ds(begin, half), :], buffer.at[at], arrivals.at[chunk])
        load.start()
        copies.append((load, pltpu.make_async_copy(buffer.at[at], sliced.at[at], departures.at[chunk])))
    for load, store in copies:
        load.wait()
        store.start()
    for _, store in copies:
        store.wait()


def slice_pairs(pairs, half):
    shape = (pairs.shape[0], half, pairs.shape[2])
    hbm = pl.BlockSpec(memory_space=pl.ANY)
    return pl.pallas_call(
        slice_kernel,
        in_specs=[hbm],
        out_specs=hbm,
        out_shape=jax.ShapeDtypeStruct(shape, bf16),
        scratch_shapes=[
            pltpu.VMEM(shape, bf16),
            pltpu.SemaphoreType.DMA((CHUNKS,)),
            pltpu.SemaphoreType.DMA((CHUNKS,)),
        ],
        compiler_params=params(63),
        cost_estimate=cost(3),
        name="slice_pairs",
    )(pairs)


def project_kernel(
    blocks,
    place,
    point_own,
    chain_own,
    query_nodes,
    query_angles,
    query_trans,
    query_chain,
    key_angles,
    key_trans,
    key_chain,
    query_weight_own,
    key_weight_own,
    bias_own,
    packed,
    edge_key_weight,
    *rest,
):
    key_blocks = rest[:blocks]
    scores, values, bias_spread, query_frames, edge_keys = rest[blocks : blocks + 5]
    keys, key_proj, query_proj, key_side, query_side, query_rows = rest[blocks + 5 :]
    sub, mine = place[0], place[1]
    local_heads = query_weight_own.shape[0] // QCOLS
    query_count, key_count = query_nodes.shape[0], keys.shape[0]
    half = scores.shape[1]
    share = key_blocks[0].shape[0]
    query_at = up16(local_heads * KCOLS)
    last_at = query_at + up16(local_heads * QCOLS)
    last = packed[last_at : last_at + 16].astype(f32)
    bias_other = last[0:local_heads, : bias_own.shape[1]].astype(bf16)
    gains = last[:, bias_own.shape[1] :]
    point_other = gains[:, 0:1] + gains[:, 1:2] + gains[:, 2:3]
    chain_other = gains[:, 3:4] + gains[:, 4:5] + gains[:, 5:6]
    rows = (blocks + 1) // 2
    arrived = [key_blocks[0][...], packed[last_at + 16 :], *(block[...] for block in key_blocks[1:])]
    for step, block in enumerate(arrived):
        source = 2 * lax.rem(mine - step // 2 + rows, rows) + (1 - sub if step % 2 else sub)
        keys[pl.ds(pl.multiple_of(source * share, share), share), :] = block
    nodes = keys[...]
    key_proj[0] = dot_nt(key_weight_own[...], nodes)
    key_proj[1] = dot_nt(packed[: local_heads * KCOLS], nodes)
    query_proj[0] = dot_nt(query_weight_own[...], query_nodes[...])
    query_proj[1] = dot_nt(packed[query_at : query_at + local_heads * QCOLS], query_nodes[...])
    edge_keys[...] = dot_tt(edge_key_weight[...], nodes)

    channels = bias_own.shape[1] // 2
    spread = channels * ROWS
    for at, offset in enumerate((sub * channels, (1 - sub) * channels)):
        select = (iota((2 * channels, spread), 0) == offset + iota((2 * channels, spread), 1) // ROWS)
        select = select.astype(f32).astype(bf16)
        diagonal = iota((1, ROWS, spread), 1) == iota((1, ROWS, spread), 2) % ROWS
        for which, weight in enumerate((bias_own[...], bias_other)):
            row = dot(weight, select)
            block = jnp.where(diagonal, row[:, None, :], 0.0).reshape(local_heads * ROWS, spread)
            begin = which * local_heads * ROWS
            bias_spread[begin : begin + local_heads * ROWS, at * spread : (at + 1) * spread] = block.astype(bf16)

    key_frames = rotation_rows(key_angles[...])
    query_rotation = rotation_rows(query_angles[...])
    frame_rows = [query_rotation[a][b] for a in range(3) for b in range(3)]
    frame_rows += [query_trans[a : a + 1, :] for a in range(3)]
    frame_rows += [query_chain[...].astype(f32)] + [jnp.zeros((1, query_count), f32)] * 3
    query_frames[...] = jnp.concatenate(frame_rows, axis=0).T
    centre = jnp.mean(query_trans[...], axis=1, keepdims=True)

    key_side[...] = jnp.zeros_like(key_side)
    query_side[...] = jnp.zeros_like(query_side)
    key_squares = []
    for head in range(2 * local_heads):
        which, at = divmod(head, local_heads)
        scale = (point_own[at] if which == 0 else point_other[at : at + 1]) * point_factor
        begin = at * KCOLS
        key_side[head, 0:CH] = rounded(key_proj[which, begin : begin + CH])
        values[head, 0:CH] = key_proj[which, begin + CH : begin + 2 * CH].astype(bf16)
        begin += 2 * CH
        local = [key_proj[which, begin + PQ * b : begin + PQ * (b + 1)] for b in range(3)]
        squares = jnp.zeros((1, key_count), f32)
        for a in range(3):
            moved = sum(key_frames[a][b] * local[b] for b in range(3)) + (
                key_trans[a : a + 1, :] - centre[a : a + 1]
            )
            squares = squares + jnp.sum(moved * moved, axis=0, keepdims=True)
            high = rounded(moved)
            key_side[head, CH + PQ * a : CH + PQ * (a + 1)] = high
            key_side[head, CH + PQ * (3 + a) : CH + PQ * (4 + a)] = moved - high
            key_side[head, CH + PQ * (6 + a) : CH + PQ * (7 + a)] = high
        key_squares.append(squares)
        begin += 3 * PQ
        local = [key_proj[which, begin + PV * b : begin + PV * (b + 1)] for b in range(3)]
        highs, lows = [], []
        for a in range(3):
            moved = sum(key_frames[a][b] * local[b] for b in range(3)) + key_trans[a : a + 1, :]
            highs.append(rounded(moved))
            lows.append(moved - highs[-1])
        values[head, CH : CH + 3 * PV] = jnp.concatenate(highs, axis=0).astype(bf16)
        values[head, CH + 3 * PV : CH + 6 * PV] = jnp.concatenate(lows, axis=0).astype(bf16)
        begin = at * QCOLS
        query_side[head, 0:CH] = rounded(query_proj[which, begin : begin + CH]) * (1.0 / math.sqrt(CH))
        begin += CH
        local = [query_proj[which, begin + PQ * b : begin + PQ * (b + 1)] for b in range(3)]
        squares = jnp.zeros((1, query_count), f32)
        for a in range(3):
            moved = sum(query_rotation[a][b] * local[b] for b in range(3)) + (
                query_trans[a : a + 1, :] - centre[a : a + 1]
            )
            squares = squares + jnp.sum(moved * moved, axis=0, keepdims=True)
            moved = moved * (2.0 * scale)
            high = rounded(moved)
            query_side[head, CH + PQ * a : CH + PQ * (a + 1)] = high
            query_side[head, CH + PQ * (3 + a) : CH + PQ * (4 + a)] = high
            query_side[head, CH + PQ * (6 + a) : CH + PQ * (7 + a)] = moved - high
        query_side[head, SLOT - 1 : SLOT] = squares * (-scale)
    for head in range(2 * local_heads):
        query_rows[head] = query_side[head].T
    begin = pl.multiple_of(sub * half, half)
    chains = query_frames[pl.ds(begin, half), 12:13]
    same = (chains == key_chain[...].astype(f32)).astype(f32)
    for head in range(2 * local_heads):
        which, at = divmod(head, local_heads)
        scale = (point_own[at] if which == 0 else point_other[at : at + 1]) * point_factor
        chain_gain = chain_own[at] if which == 0 else chain_other[at : at + 1]
        left = query_rows[head, pl.ds(begin, half), :]
        score = dot(left.astype(bf16), key_side[head].astype(bf16))
        score = score + left[:, SLOT - 1 : SLOT] - scale * key_squares[head] + chain_gain * same
        scores[head] = linear_scale * score


def project(
    place, gains, query_side, key_side, query_weight, key_weight, bias_weight, packed, edge_key_weight, key_blocks, half
):
    query_count = query_side[0].shape[0]
    key_count = key_side[0].shape[1]
    local_heads = gains[0].shape[0]
    heads = 2 * local_heads
    channels, hidden = bias_weight.shape[1], edge_key_weight.shape[1]
    operands = [*query_side, *key_side, query_weight, key_weight, bias_weight, packed, edge_key_weight, *key_blocks]
    return pl.pallas_call(
        functools.partial(project_kernel, len(key_blocks)),
        in_specs=[SMEM] * 3 + [whole(a) for a in operands],
        out_shape=(
            jax.ShapeDtypeStruct((heads, half, key_count), f32),
            jax.ShapeDtypeStruct((heads, SLOT, key_count), bf16),
            jax.ShapeDtypeStruct((heads * ROWS, channels * ROWS), bf16),
            jax.ShapeDtypeStruct((query_count, 16), f32),
            jax.ShapeDtypeStruct((hidden, key_count), f32),
        ),
        scratch_shapes=[
            pltpu.VMEM((key_count, query_side[0].shape[1]), bf16),
            pltpu.VMEM((2, local_heads * KCOLS, key_count), f32),
            pltpu.VMEM((2, local_heads * QCOLS, query_count), f32),
            pltpu.VMEM((heads, SLOT, key_count), f32),
            pltpu.VMEM((heads, SLOT, query_count), f32),
            pltpu.VMEM((heads, query_count, SLOT), f32),
        ],
        compiler_params=params(63),
        cost_estimate=cost(12),
        name="project",
    )(place, *gains, *operands)


def attend_kernel(
    targets,
    place,
    base_scores,
    values,
    bias_spread,
    frames,
    mask,
    own_pairs,
    other_pairs,
    *rest,
):
    results = rest[:targets]
    part, weight_high, weight_low, peaks, sums, gather_own, gather_other = rest[targets:]
    step = pl.program_id(0)
    sub = place[0]
    heads, _, keys = base_scores.shape
    channels = own_pairs.shape[0]
    spread = channels * ROWS
    lanes = 2 * channels

    @pl.when(step == 0)
    def _():
        source = iota((spread, lanes), 0) // ROWS
        target = iota((spread, lanes), 1)
        gather_own[...] = (target == source + sub * channels).astype(f32).astype(bf16)
        gather_other[...] = (target == source + (1 - sub) * channels).astype(f32).astype(bf16)

    rows = own_pairs.shape[1]
    diagonal = iota((heads * ROWS, spread), 0) % ROWS == iota((heads * ROWS, spread), 1) % ROWS
    blocks = []
    for begin in range(0, rows, ROWS):
        span = slice(begin, begin + ROWS)
        own = own_pairs[:, span, :].reshape(spread, keys)
        other = other_pairs[:, span, :].reshape(spread, keys)
        bias = dot(bias_spread[:, :spread], own) + dot(bias_spread[:, spread:], other)
        score = base_scores[:, span, :] + linear_scale * bias.reshape(heads, ROWS, keys)
        score = jnp.where(mask[span, :][None] == 1, score, masked_score)
        peak = jnp.max(score, axis=2, keepdims=True)
        weight = jnp.exp(score - peak)
        total = jnp.sum(weight, axis=2, keepdims=True)
        high = weight.astype(bf16)
        at = pl.ds(pl.multiple_of(step * rows + begin, ROWS), ROWS)
        weight_high[:, at, :] = high
        weight_low[:, at, :] = (weight - high.astype(f32)).astype(bf16)
        peaks[:, at, :] = jnp.broadcast_to(peak, (heads, ROWS, lanes))
        sums[:, at, :] = jnp.broadcast_to(total, (heads, ROWS, lanes))
        blocks.append((at, own, other, high.reshape(heads * ROWS, keys), (1.0 / total).reshape(heads * ROWS, 1)))
    for at, own, other, flat, scale in blocks:
        own_part = jnp.where(diagonal, dot_nt(flat, own) * scale, 0.0).astype(bf16)
        other_part = jnp.where(diagonal, dot_nt(flat, other) * scale, 0.0).astype(bf16)
        pairs = dot(own_part, gather_own[...]) + dot(other_part, gather_other[...])
        part[0:heads, at, :] = pairs.reshape(heads, ROWS, lanes).astype(bf16)

    @pl.when(step == pl.num_programs(0) - 1)
    def _():
        half = frames.shape[0]
        lane = iota((half, 2 * SLOT), 1)
        first = lane < SLOT
        slot = lane % SLOT
        plane = (slot - CH) // PV
        inside = (slot >= CH) & (slot < CH + 3 * PV)

        def on_planes(columns):
            out = jnp.zeros((half, 2 * SLOT), f32)
            for b, column in columns:
                out = jnp.where(inside & (plane == b), frames[:, column : column + 1], out)
            return out

        shift = on_planes([(a, 9 + a) for a in range(3)])
        turns = [
            (d, on_planes([(b, 3 * (b - d) + b) for b in range(3) if 0 <= b - d < 3])) for d in range(-2, 3)
        ]
        for pair in range(heads // 2):
            a, b = 2 * pair, 2 * pair + 1
            left = jnp.concatenate([weight_high[a], weight_low[a], weight_high[b], weight_low[b]], axis=0)
            right = jnp.concatenate([values[a], values[b]], axis=0)
            out = dot_nt(left, right)
            upper = jnp.where(first, out[0:half], out[2 * half : 3 * half])
            lower = jnp.where(first, out[half : 2 * half], out[3 * half :])
            peak_pair = jnp.where(first, peaks[a], peaks[b])
            sum_pair = jnp.where(first, sums[a], sums[b])
            inverse = 1.0 / sum_pair
            points = (upper + lower + pltpu.roll(upper, 2 * SLOT - 3 * PV, 1)) * inverse - shift
            turned = jnp.zeros((half, 2 * SLOT), f32)
            for d, factor in turns:
                turned = turned + factor * (pltpu.roll(points, (d * PV) % (2 * SLOT), 1) if d else points)
            result = jnp.where(slot < CH, upper * inverse, turned)
            at = CH + 3 * PV
            for value in (peak_pair, sum_pair):
                for _ in range(3):
                    piece = rounded(value)
                    result = jnp.where(slot == at, piece, result)
                    value = value - piece
                    at += 1
            part[heads + pair] = jnp.where(slot < at, result, 0.0).astype(bf16)
        share = half // targets
        for target in range(targets):
            at = jnp.bitwise_xor(place[2], target) * share if targets > 1 else 0
            results[target][...] = part[:, pl.ds(pl.multiple_of(at, share) if targets > 1 else 0, share), :]


def attend(place, own_pairs, other_pairs, base_scores, mask, values, bias_spread, frames, targets):
    heads, half, keys = base_scores.shape
    channels = own_pairs.shape[0]
    rows = math.gcd(half, ATTEND_ROWS)
    steps = half // rows
    pair_block = pl.BlockSpec((channels, rows, keys), lambda g, p: (0, p[0] * steps + g, 0))
    slots = heads + heads // 2
    return pl.pallas_call(
        functools.partial(attend_kernel, targets),
        grid_spec=pltpu.PrefetchScalarGridSpec(
            num_scalar_prefetch=1,
            grid=(steps,),
            in_specs=[
                pl.BlockSpec((heads, rows, keys), lambda g, p: (0, g, 0)),
                whole(values),
                whole(bias_spread),
                pl.BlockSpec((half, frames.shape[1]), lambda g, p: (p[0], 0)),
                pl.BlockSpec((rows, keys), lambda g, p: (p[0] * steps + g, 0)),
                pair_block,
                pl.BlockSpec((channels, rows, keys), lambda g, p: (0, g, 0)),
            ],
            out_specs=[pl.BlockSpec((slots, half // targets, 2 * channels), lambda g, p: (0, 0, 0))] * targets,
            scratch_shapes=[
                pltpu.VMEM((slots, half, 2 * channels), bf16),
                pltpu.VMEM((heads, half, keys), bf16),
                pltpu.VMEM((heads, half, keys), bf16),
                pltpu.VMEM((heads, half, 2 * channels), f32),
                pltpu.VMEM((heads, half, 2 * channels), f32),
                pltpu.VMEM((channels * ROWS, 2 * channels), bf16),
                pltpu.VMEM((channels * ROWS, 2 * channels), bf16),
            ],
        ),
        out_shape=[jax.ShapeDtypeStruct((slots, half // targets, 2 * channels), bf16)] * targets,
        compiler_params=params(63),
        cost_estimate=cost(9),
        name="attend",
    )(place, base_scores, values, bias_spread, frames, mask, own_pairs, other_pairs)


def norm(values, gain):
    centred = values - jnp.mean(values, axis=-1, keepdims=True)
    variance = jnp.mean(centred * centred, axis=-1, keepdims=True)
    return centred * lax.rsqrt(variance + norm_epsilon) * gain


def node_kernel(
    count,
    place,
    nodes,
    out_own,
    out_other,
    first_gain,
    second_gain,
    gate_weight,
    up_weight,
    down_weight,
    *rest,
):
    parts, result = rest[:count], rest[count]
    heads = parts[0].shape[0] * 2 // 3
    rows, lanes = parts[0].shape[1:]
    local_heads = heads // 2
    tall = local_heads * rows
    first = iota((tall, lanes), 1) < SLOT
    slot = iota((tall, lanes), 1) % SLOT
    at = CH + 3 * PV

    def broadcast(values, lane):
        return jnp.where(
            first,
            jnp.broadcast_to(values[:, lane : lane + 1], (tall, lanes)),
            jnp.broadcast_to(values[:, SLOT + lane : SLOT + lane + 1], (tall, lanes)),
        )

    extras, peaks, sums = [], [], []
    for part in parts:
        extra = part[heads:].astype(f32).reshape(tall, lanes)
        joined = extra + pltpu.roll(extra, lanes - 1, 1) + pltpu.roll(extra, lanes - 2, 1)
        extras.append(extra)
        peaks.append(broadcast(joined, at))
        sums.append(broadcast(joined, at + 3))
    peak = functools.reduce(jnp.maximum, peaks)
    shares = [s * jnp.exp(p - peak) for s, p in zip(sums, peaks)]
    total = sum(shares)
    shares = [s / total for s in shares]
    merged = sum(s * e for s, e in zip(shares, extras))
    squares = merged * merged
    norms = jnp.sqrt(
        1.0 + pltpu.roll(squares, PV, 1) + pltpu.roll(squares, 2 * PV, 1) + pltpu.roll(squares, 3 * PV, 1)
    )
    merged = jnp.where(slot < at, merged, norms).astype(bf16)
    projected = jnp.zeros((rows, nodes.shape[1]), f32)
    for head in range(heads):
        pair, odd = divmod(head, 2)
        weight = out_own if head < local_heads else out_other
        begin = (head % local_heads) * (FEATURES + lanes)
        span = slice(pair * rows, (pair + 1) * rows)
        lane = odd * SLOT
        mixed = jnp.zeros((rows, lanes), f32)
        for share, part in zip(shares, parts):
            factor = jnp.broadcast_to(share[span, lane : lane + 1], (rows, lanes))
            mixed = mixed + factor * part[head].astype(f32)
        projected = projected + dot(mixed.astype(bf16), weight[begin + FEATURES : begin + FEATURES + lanes])
        projected = projected + dot(merged[span, lane : lane + FEATURES], weight[begin : begin + FEATURES])
    own = nodes[pl.ds(pl.multiple_of(place[0], ROWS), rows), :]
    first_nodes = norm(own.astype(f32) + projected, first_gain[...])
    first_rounded = first_nodes.astype(bf16)
    gate = dot(first_rounded, gate_weight[...])
    hidden = (gate / (1.0 + jnp.exp(-gate)) * dot(first_rounded, up_weight[...])).astype(bf16)
    result[...] = norm(first_nodes + dot(hidden, down_weight[...]), second_gain[...]).astype(bf16)


def update_nodes(place, parts, nodes, out_own, out_other, first_gain, second_gain, gate_weight, up_weight, down_weight):
    operands = [nodes, out_own, out_other, first_gain, second_gain, gate_weight, up_weight, down_weight, *parts]
    return pl.pallas_call(
        functools.partial(node_kernel, len(parts)),
        in_specs=[SMEM] + [whole(a) for a in operands],
        out_shape=jax.ShapeDtypeStruct((parts[0].shape[1], nodes.shape[1]), bf16),
        compiler_params=params(16),
        cost_estimate=cost(2),
        name="nodes",
    )(place, *operands)


def turn_kernel(place, own_pairs, other_pairs, in_weight, out_weight, result, left, out_left):
    channels = own_pairs.shape[0]
    sub = place[0]

    @pl.when(pl.program_id(0) == 0)
    def _():
        own = pl.multiple_of(sub * channels, channels)
        other = pl.multiple_of((1 - sub) * channels, channels)
        left[:, 0:channels] = in_weight[pl.ds(own, channels), :].astype(f32).T.astype(bf16)
        left[:, channels:] = in_weight[pl.ds(other, channels), :].astype(f32).T.astype(bf16)
        flipped = out_weight[...].astype(f32).T
        out_left[0:channels] = jnp.where(sub == 0, flipped[0:channels], flipped[channels:]).astype(bf16)
        out_left[channels:] = jnp.where(sub == 0, flipped[channels:], flipped[0:channels]).astype(bf16)

    result[:, 0:channels, :] = jnp.swapaxes(own_pairs[...], 0, 1)
    result[:, channels:, :] = jnp.swapaxes(other_pairs[...], 0, 1)


def turn_pairs(place, own_pairs, other_pairs, in_weight, out_weight, half):
    channels, _, keys = other_pairs.shape
    both, hidden = in_weight.shape
    rows = math.gcd(half, TURN_ROWS)
    steps = half // rows
    return pl.pallas_call(
        turn_kernel,
        grid_spec=pltpu.PrefetchScalarGridSpec(
            num_scalar_prefetch=1,
            grid=(steps,),
            in_specs=[
                pl.BlockSpec((channels, rows, keys), lambda g, p: (0, p[0] * steps + g, 0)),
                pl.BlockSpec((channels, rows, keys), lambda g, p: (0, g, 0)),
                whole(in_weight),
                whole(out_weight),
            ],
            out_specs=(
                pl.BlockSpec((rows, both, keys), lambda g, p: (g, 0, 0)),
                pl.BlockSpec((hidden, both), lambda g, p: (0, 0)),
                pl.BlockSpec((both, hidden), lambda g, p: (0, 0)),
            ),
        ),
        out_shape=(
            jax.ShapeDtypeStruct((half, both, keys), bf16),
            jax.ShapeDtypeStruct((hidden, both), bf16),
            jax.ShapeDtypeStruct((both, hidden), bf16),
        ),
        compiler_params=params(16),
        cost_estimate=cost(4),
        name="turn_pairs",
    )(place, own_pairs, other_pairs, in_weight, out_weight)


def edge_kernel(count, place, turned, *rest):
    ring = rest[:count]
    edge_keys, in_left, out_left, query_weight, kept, sent, new_nodes, nodes, left, picks, hidden, fresh = rest[count:]
    step, rows = pl.program_id(0), ROWS
    _, both, keys = turned.shape
    channels = both // 2

    @pl.when(pl.program_id(0) == 0)
    def _():
        at = 0
        for source in ring:
            for begin in range(0, source.shape[0], rows):
                nodes[at] = source[begin : begin + rows]
                at += 1
        for span in range(left.shape[0]):
            left[span, :, 0:both] = in_left[...]
        chosen = iota((rows, 2 * rows, keys), 1) % rows == iota((rows, 2 * rows, keys), 0)
        picks[...] = chosen.astype(f32).astype(bf16)

    spans = turned.shape[0] // rows
    for span in range(spans):
        begin = span * rows
        own = nodes[jnp.bitwise_xor(step * spans + span, place[1])]
        queries = dot_tt(query_weight[...], own)
        high = queries.astype(bf16)
        left[span, :, both : both + rows] = high
        left[span, :, both + rows :] = (queries - high.astype(f32)).astype(bf16)
        new_nodes[begin : begin + rows] = own
        for at in range(sent.shape[0] - channels):
            sent[channels + at, begin : begin + rows] = own[:, at * keys : (at + 1) * keys]
    for row in range(spans * rows):
        right = jnp.concatenate([turned[row], picks[row % rows]], axis=0)
        hidden[row] = jnp.maximum(dot(left[row // rows], right) + edge_keys[...], 0.0).astype(bf16)
    for row in range(spans * rows):
        old = turned[row].astype(f32)
        fresh[row] = (old + dot(out_left[...], hidden[row])).astype(bf16)
    kept[...] = jnp.swapaxes(fresh[:, 0:channels, :], 0, 1)
    sent[0:channels] = jnp.swapaxes(fresh[:, channels:, :], 0, 1)


def update_pairs(place, count, turned, ring, edge_keys, in_left, out_left, query_weight):
    half, both, keys = turned.shape
    channels, hidden = both // 2, in_left.shape[0]
    rows, features = math.gcd(half, EDGE_ROWS), ring[0].shape[1]
    steps = half // rows
    assert features % keys == 0
    extra = features // keys
    return pl.pallas_call(
        functools.partial(edge_kernel, len(ring)),
        grid_spec=pltpu.PrefetchScalarGridSpec(
            num_scalar_prefetch=1,
            grid=(steps,),
            in_specs=[
                pl.BlockSpec((rows, both, keys), lambda g, p: (g, 0, 0)),
                *[whole(a) for a in ring],
                whole(edge_keys),
                whole(in_left),
                whole(out_left),
                whole(query_weight),
            ],
            out_specs=(
                pl.BlockSpec((channels, rows, keys), lambda g, p: (0, p[0] * steps + g, 0)),
                pl.BlockSpec((channels + extra, rows, keys), lambda g, p: (0, g, 0)),
                pl.BlockSpec((rows, features), lambda g, p: (p[0] * steps + g, 0)),
            ),
            scratch_shapes=[
                pltpu.VMEM((half // ROWS, ROWS, features), bf16),
                pltpu.VMEM((rows // ROWS, hidden, both + 2 * ROWS), bf16),
                pltpu.VMEM((ROWS, 2 * ROWS, keys), bf16),
                pltpu.VMEM((rows, hidden, keys), bf16),
                pltpu.VMEM((rows, both, keys), bf16),
            ],
        ),
        out_shape=(
            jax.ShapeDtypeStruct((channels, count, keys), bf16),
            jax.ShapeDtypeStruct((channels + extra, half, keys), bf16),
            jax.ShapeDtypeStruct((count, features), bf16),
        ),
        compiler_params=params(20),
        cost_estimate=cost(8),
        name="edges",
    )(place, turned, *ring, edge_keys, in_left, out_left, query_weight)


def finish_kernel(arrived, pairs_in, nodes_in, pairs, nodes, sems):
    channels, half, keys = pairs.shape[0], arrived.shape[1], arrived.shape[2]
    begin = pl.multiple_of((1 - lax.axis_index("sub")) * half, half)
    rows = pl.ds(begin, half)
    copies = [pltpu.make_async_copy(arrived.at[0:channels], pairs.at[:, rows, :], sems.at[0])]
    for at in range(arrived.shape[0] - channels):
        target = nodes.at[rows, at * keys : (at + 1) * keys]
        copies.append(pltpu.make_async_copy(arrived.at[channels + at], target, sems.at[1 + at]))
    for copy in copies:
        copy.start()
    for copy in copies:
        copy.wait()


def finish(arrived, pairs, nodes):
    hbm = pl.BlockSpec(memory_space=pl.ANY)
    return pl.pallas_call(
        finish_kernel,
        in_specs=[whole(arrived), hbm, hbm],
        out_specs=(hbm, hbm),
        out_shape=(
            jax.ShapeDtypeStruct(pairs.shape, bf16),
            jax.ShapeDtypeStruct(nodes.shape, bf16),
        ),
        scratch_shapes=[pltpu.SemaphoreType.DMA((1 + arrived.shape[0] - pairs.shape[0],))],
        input_output_aliases={1: 0, 2: 1},
        compiler_params=params(8),
        cost_estimate=cost(1),
        name="finish",
    )(arrived, pairs, nodes)


def shards(
    node_query,
    query_angles,
    query_trans,
    query_chain,
    node_key,
    key_angles,
    key_trans,
    key_chain,
    pair_features,
    pair_mask,
    query_weight,
    key_weight,
    bias_weight,
    point_gain,
    chain_gain,
    out_weight,
    first_gain,
    second_gain,
    gate_weight,
    up_weight,
    down_weight,
    edge_query_weight,
    edge_key_weight,
    edge_in_weight,
    edge_out_weight,
):
    subs, cols, rows = lax.axis_size("sub"), lax.axis_size("col"), lax.axis_size("row")
    sub, col = lax.axis_index("sub"), lax.axis_index("col")

    def swap(values):
        return lax.ppermute(values, "sub", [(i, (i + 1) % subs) for i in range(subs)])

    def step(by_row, by_sub):
        return [
            (r * subs + c, (r + by_row) % rows * subs + (c + by_sub) % subs) for r in range(rows) for c in range(subs)
        ]

    key_blocks = [node_key] + [
        lax.ppermute(node_key, ("row", "sub"), step(r, c)) for r in range(1, rows) for c in range(subs)
    ]
    half = node_query.shape[0] // subs
    query_weight, key_weight, bias_weight = query_weight.T, key_weight.T, bias_weight.T
    packed = pack(point_gain, chain_gain, key_weight, query_weight, bias_weight, node_key)
    packed, late_pairs = lax.optimization_barrier((swap(packed), pair_features))
    far_pairs, key_blocks = lax.optimization_barrier((slice_pairs(late_pairs, half), key_blocks))
    other_pairs = swap(far_pairs)
    place = jnp.stack([sub, lax.axis_index("row"), col]).astype(jnp.int32)

    share = half // cols
    assert cols & (cols - 1) == 0
    spare = -share % ROWS
    base_scores, values, bias_spread, frames, edge_keys = project(
        place,
        [point_gain, chain_gain],
        [node_query, query_angles, query_trans, query_chain[None, :]],
        [key_angles, key_trans, key_chain[None, :]],
        query_weight,
        key_weight,
        bias_weight,
        packed,
        edge_key_weight,
        key_blocks,
        half,
    )
    targets = 1 if spare else cols
    pieces = attend(
        place, pair_features, other_pairs, base_scores, pair_mask, values, bias_spread, frames, targets
    )
    other_out = swap(lax.optimization_barrier((out_weight, base_scores))[0])
    if spare:
        pieces = [
            lax.dynamic_slice_in_dim(pieces[0], jnp.bitwise_xor(col, k) * share, share, 1) for k in range(cols)
        ]
    def meet(values, k):
        return lax.ppermute(values, "col", [(i, i ^ k) for i in range(cols)])

    order = range(cols - 1, 0, -1)
    met = {k: meet(pieces[k], k) for k in order}
    parts = [pieces[0]] + [met[k] for k in order]
    own_nodes, begin = node_query, sub * half + col * share
    if spare:
        own_nodes, begin = lax.dynamic_slice_in_dim(node_query, begin, share, 0), 0 * begin
        parts = [jnp.pad(p, ((0, 0), (0, spare), (0, 0))) for p in parts]
        own_nodes = jnp.pad(own_nodes, ((0, spare), (0, 0)))
    turn_place, _ = lax.optimization_barrier((place, pieces))
    turned, in_left, out_left = turn_pairs(
        turn_place, pair_features, other_pairs, edge_in_weight, edge_out_weight, half
    )
    own_nodes, turned = lax.optimization_barrier((own_nodes, turned))
    fresh_nodes = update_nodes(
        begin.astype(jnp.int32).reshape(1),
        parts,
        own_nodes,
        out_weight,
        other_out,
        first_gain[None, :],
        second_gain[None, :],
        gate_weight,
        up_weight,
        down_weight,
    )[:share]
    met = {k: meet(fresh_nodes, k) for k in order}
    ring = [fresh_nodes] + [met[k] for k in range(1, cols)]
    per_share = max(share // ROWS, 1)
    turn = col * per_share
    if spare:
        ring = [jnp.stack(ring)[jnp.bitwise_xor(jnp.arange(cols), col)].reshape(half, node_query.shape[1])]
        turn = 0 * col
    edge_place = jnp.stack([sub, turn]).astype(jnp.int32)
    kept, sent, new_nodes = update_pairs(
        edge_place, pair_features.shape[1], turned, ring, edge_keys, in_left, out_left, edge_query_weight
    )
    updated_pairs, updated_nodes = finish(swap(sent), kept, new_nodes)
    return (updated_nodes, updated_pairs)


def solution(mesh):
    return jax.shard_map(
        shards,
        mesh=mesh,
        in_specs=(
            P(("rep", "row"), None),
            P(None, ("rep", "row")),
            P(None, ("rep", "row")),
            P(("rep", "row")),
            P(("rep", "col", "row", "sub"), None),
            P(None, ("rep", "col")),
            P(None, ("rep", "col")),
            P(("rep", "col")),
            P("sub", ("rep", "row"), "col"),
            P(("rep", "row"), "col"),
            P(None, "sub"),
            P(None, "sub"),
            P(None, "sub"),
            P("sub"),
            P("sub"),
            P("sub", None),
            P(),
            P(),
            P(),
            P(),
            P(),
            P(),
            P(),
            P(),
            P(),
        ),
        out_specs=(P(("rep", "row"), None), P("sub", ("rep", "row"), "col")),
        check_vma=False,
    )
```

```python
import functools
import math

import jax
import jax.numpy as jnp
from jax import lax
from jax.experimental import pallas as pl
from jax.experimental.pallas import tpu as pltpu
from jax.sharding import PartitionSpec as P

CH = 16
PQ = 4
PV = 8
QCOLS = CH + 3 * PQ
KCOLS = 2 * CH + 3 * PQ + 3 * PV
FEATURES = CH + 4 * PV
SLOT = 64
ROWS = 16
VMEM_MIB = 60
ATTEND_ROWS = 32
TURN_ROWS = 32
EDGE_ROWS = 32

linear_scale = math.sqrt(1.0 / 3.0)
masked_score = -1000000000.0
norm_epsilon = 1e-05
point_factor = math.sqrt(2.0 / (9.0 * PQ)) / 2.0

f32 = jnp.float32
bf16 = jnp.bfloat16


def params(mib):
    return pltpu.CompilerParams(vmem_limit_bytes=mib * 2**20)


def cost(microseconds):
    return pl.CostEstimate(flops=0, bytes_accessed=3_000_000 * microseconds, transcendentals=0)


def dot(left, right):
    return jnp.dot(left, right, preferred_element_type=f32)


def dot_nt(left, right):
    return lax.dot_general(left, right, (((1,), (1,)), ((), ())), preferred_element_type=f32)


def dot_tn(left, right):
    return lax.dot_general(left, right, (((0,), (0,)), ((), ())), preferred_element_type=f32)


def dot_tt(left, right):
    return lax.dot_general(left, right, (((0,), (1,)), ((), ())), preferred_element_type=f32)


def iota(shape, axis):
    return lax.broadcasted_iota(jnp.int32, shape, axis)


def rounded(values):
    return values.astype(bf16).astype(f32)


def rotation_rows(angles):
    cos, sin = jnp.cos(angles), jnp.sin(angles)
    cy, cp, cr = cos[0:1], cos[1:2], cos[2:3]
    sy, sp, sr = sin[0:1], sin[1:2], sin[2:3]
    return [
        [cy * cp, cy * sp * sr - sy * cr, cy * sp * cr + sy * sr],
        [sy * cp, sy * sp * sr + cy * cr, sy * sp * cr - cy * sr],
        [-sp, cp * sr, cp * cr],
    ]


def whole(array):
    return pl.BlockSpec(array.shape, lambda *_: (0,) * array.ndim)


SMEM = pl.BlockSpec(memory_space=pltpu.SMEM)


def up16(count):
    return -(-count // 16) * 16


def pack_kernel(point_gain, chain_gain, key_weight, query_weight, bias_weight, nodes, packed, last):
    heads, channels = bias_weight.shape
    at = up16(key_weight.shape[0])
    end = at + up16(query_weight.shape[0])
    packed[0 : key_weight.shape[0]] = key_weight[...]
    packed[at : at + query_weight.shape[0]] = query_weight[...]
    row, lane = iota((16, 128), 0), iota((16, 128), 1)
    pieces = jnp.zeros((16, 128), f32)
    for which, gain in enumerate((point_gain, chain_gain)):
        value = jnp.zeros((16, 128), f32)
        for head in range(heads):
            value = jnp.where(row == head, gain[head], value)
        for step in range(3):
            piece = rounded(value)
            pieces = jnp.where(lane == 3 * which + step, piece, pieces)
            value = value - piece
    last[...] = jnp.zeros_like(last)
    last[0:heads, 0:channels] = bias_weight[...].astype(f32)
    last[:, channels : channels + 128] = pieces
    packed[end : end + 16] = last[...].astype(bf16)
    packed[end + 16 :] = nodes[...]


def pack(point_gain, chain_gain, key_weight, query_weight, bias_weight, nodes):
    operands = [key_weight, query_weight, bias_weight, nodes]
    total = up16(key_weight.shape[0]) + up16(query_weight.shape[0]) + 16 + nodes.shape[0]
    return pl.pallas_call(
        pack_kernel,
        in_specs=[SMEM] * 2 + [whole(a) for a in operands],
        out_shape=jax.ShapeDtypeStruct((total, key_weight.shape[1]), bf16),
        scratch_shapes=[pltpu.VMEM((16, key_weight.shape[1]), f32)],
        compiler_params=params(63),
        cost_estimate=cost(10),
        name="pack",
    )(point_gain, chain_gain, *operands)


def project_kernel(
    blocks,
    place,
    point_own,
    chain_own,
    query_nodes,
    query_angles,
    query_trans,
    query_chain,
    key_angles,
    key_trans,
    key_chain,
    query_weight_own,
    key_weight_own,
    bias_own,
    packed,
    edge_key_weight,
    *rest,
):
    key_blocks = rest[:blocks]
    scores, values, bias_spread, query_frames, edge_keys = rest[blocks : blocks + 5]
    keys, key_proj, query_proj, key_side, query_side, query_rows = rest[blocks + 5 :]
    sub, mine = place[0], place[1]
    local_heads = query_weight_own.shape[0] // QCOLS
    query_count, key_count = query_nodes.shape[0], keys.shape[0]
    half = scores.shape[1]
    share = key_blocks[0].shape[0]
    query_at = up16(local_heads * KCOLS)
    last_at = query_at + up16(local_heads * QCOLS)
    last = packed[last_at : last_at + 16].astype(f32)
    bias_other = last[0:local_heads, : bias_own.shape[1]].astype(bf16)
    gains = last[:, bias_own.shape[1] :]
    point_other = gains[:, 0:1] + gains[:, 1:2] + gains[:, 2:3]
    chain_other = gains[:, 3:4] + gains[:, 4:5] + gains[:, 5:6]
    rows = (blocks + 1) // 2
    arrived = [key_blocks[0][...], packed[last_at + 16 :], *(block[...] for block in key_blocks[1:])]
    for step, block in enumerate(arrived):
        source = 2 * lax.rem(mine - step // 2 + rows, rows) + (1 - sub if step % 2 else sub)
        keys[pl.ds(pl.multiple_of(source * share, share), share), :] = block
    nodes = keys[...]
    key_proj[0] = dot_nt(key_weight_own[...], nodes)
    key_proj[1] = dot_nt(packed[: local_heads * KCOLS], nodes)
    query_proj[0] = dot_nt(query_weight_own[...], query_nodes[...])
    query_proj[1] = dot_nt(packed[query_at : query_at + local_heads * QCOLS], query_nodes[...])
    edge_keys[...] = dot_tt(edge_key_weight[...], nodes)

    channels = bias_own.shape[1] // 2
    spread = channels * ROWS
    for at, offset in enumerate((sub * channels, (1 - sub) * channels)):
        select = (iota((2 * channels, spread), 0) == offset + iota((2 * channels, spread), 1) // ROWS)
        select = select.astype(f32).astype(bf16)
        diagonal = iota((1, ROWS, spread), 1) == iota((1, ROWS, spread), 2) % ROWS
        for which, weight in enumerate((bias_own[...], bias_other)):
            row = dot(weight, select)
            block = jnp.where(diagonal, row[:, None, :], 0.0).reshape(local_heads * ROWS, spread)
            begin = which * local_heads * ROWS
            bias_spread[begin : begin + local_heads * ROWS, at * spread : (at + 1) * spread] = block.astype(bf16)

    key_frames = rotation_rows(key_angles[...])
    query_rotation = rotation_rows(query_angles[...])
    frame_rows = [query_rotation[a][b] for a in range(3) for b in range(3)]
    frame_rows += [query_trans[a : a + 1, :] for a in range(3)]
    frame_rows += [query_chain[...].astype(f32)] + [jnp.zeros((1, query_count), f32)] * 3
    query_frames[...] = jnp.concatenate(frame_rows, axis=0).T
    centre = jnp.mean(query_trans[...], axis=1, keepdims=True)

    key_side[...] = jnp.zeros_like(key_side)
    query_side[...] = jnp.zeros_like(query_side)
    key_squares = []
    for head in range(2 * local_heads):
        which, at = divmod(head, local_heads)
        scale = (point_own[at] if which == 0 else point_other[at : at + 1]) * point_factor
        begin = at * KCOLS
        key_side[head, 0:CH] = rounded(key_proj[which, begin : begin + CH])
        values[head, 0:CH] = key_proj[which, begin + CH : begin + 2 * CH].astype(bf16)
        begin += 2 * CH
        local = [key_proj[which, begin + PQ * b : begin + PQ * (b + 1)] for b in range(3)]
        squares = jnp.zeros((1, key_count), f32)
        for a in range(3):
            moved = sum(key_frames[a][b] * local[b] for b in range(3)) + (
                key_trans[a : a + 1, :] - centre[a : a + 1]
            )
            squares = squares + jnp.sum(moved * moved, axis=0, keepdims=True)
            high = rounded(moved)
            key_side[head, CH + PQ * a : CH + PQ * (a + 1)] = high
            key_side[head, CH + PQ * (3 + a) : CH + PQ * (4 + a)] = moved - high
            key_side[head, CH + PQ * (6 + a) : CH + PQ * (7 + a)] = high
        key_squares.append(squares)
        begin += 3 * PQ
        local = [key_proj[which, begin + PV * b : begin + PV * (b + 1)] for b in range(3)]
        highs, lows = [], []
        for a in range(3):
            moved = sum(key_frames[a][b] * local[b] for b in range(3)) + key_trans[a : a + 1, :]
            highs.append(rounded(moved))
            lows.append(moved - highs[-1])
        values[head, CH : CH + 3 * PV] = jnp.concatenate(highs, axis=0).astype(bf16)
        values[head, CH + 3 * PV : CH + 6 * PV] = jnp.concatenate(lows, axis=0).astype(bf16)
        begin = at * QCOLS
        query_side[head, 0:CH] = rounded(query_proj[which, begin : begin + CH]) * (1.0 / math.sqrt(CH))
        begin += CH
        local = [query_proj[which, begin + PQ * b : begin + PQ * (b + 1)] for b in range(3)]
        squares = jnp.zeros((1, query_count), f32)
        for a in range(3):
            moved = sum(query_rotation[a][b] * local[b] for b in range(3)) + (
                query_trans[a : a + 1, :] - centre[a : a + 1]
            )
            squares = squares + jnp.sum(moved * moved, axis=0, keepdims=True)
            moved = moved * (2.0 * scale)
            high = rounded(moved)
            query_side[head, CH + PQ * a : CH + PQ * (a + 1)] = high
            query_side[head, CH + PQ * (3 + a) : CH + PQ * (4 + a)] = high
            query_side[head, CH + PQ * (6 + a) : CH + PQ * (7 + a)] = moved - high
        query_side[head, SLOT - 1 : SLOT] = squares * (-scale)
    for head in range(2 * local_heads):
        query_rows[head] = query_side[head].T
    begin = pl.multiple_of(sub * half, half)
    chains = query_frames[pl.ds(begin, half), 12:13]
    same = (chains == key_chain[...].astype(f32)).astype(f32)
    for head in range(2 * local_heads):
        which, at = divmod(head, local_heads)
        scale = (point_own[at] if which == 0 else point_other[at : at + 1]) * point_factor
        chain_gain = chain_own[at] if which == 0 else chain_other[at : at + 1]
        left = query_rows[head, pl.ds(begin, half), :]
        score = dot(left.astype(bf16), key_side[head].astype(bf16))
        score = score + left[:, SLOT - 1 : SLOT] - scale * key_squares[head] + chain_gain * same
        scores[head] = linear_scale * score


def attend_kernel(operands, key_blocks, targets, place, own_pairs, other_pairs, mask, *rest):
    inputs = rest[:operands]
    results, edge_keys = rest[operands : operands + targets], rest[operands + targets]
    scratch = rest[operands + targets + 1 :]
    part, weight_high, weight_low, peaks, sums, gather_own, gather_other = scratch[:7]
    scores, values, bias_spread, frames, *project_scratch = scratch[7:]
    step = pl.program_id(0)
    sub = place[0]
    heads, half, keys = scores.shape
    channels = own_pairs.shape[0]
    spread = channels * ROWS
    lanes = 2 * channels

    @pl.when(step == 0)
    def _():
        project_kernel(
            key_blocks, place, *inputs, scores, values, bias_spread, frames, edge_keys, *project_scratch
        )
        source = iota((spread, lanes), 0) // ROWS
        target = iota((spread, lanes), 1)
        gather_own[...] = (target == source + sub * channels).astype(f32).astype(bf16)
        gather_other[...] = (target == source + (1 - sub) * channels).astype(f32).astype(bf16)

    rows = own_pairs.shape[1]
    diagonal = iota((heads * ROWS, spread), 0) % ROWS == iota((heads * ROWS, spread), 1) % ROWS
    blocks = []
    for begin in range(0, rows, ROWS):
        span = slice(begin, begin + ROWS)
        own = own_pairs[:, span, :].reshape(spread, keys)
        other = other_pairs[:, span, :].reshape(spread, keys)
        bias = dot(bias_spread[:, :spread], own) + dot(bias_spread[:, spread:], other)
        at = pl.ds(pl.multiple_of(step * rows + begin, ROWS), ROWS)
        score = scores[:, at, :] + linear_scale * bias.reshape(heads, ROWS, keys)
        score = jnp.where(mask[span, :][None] == 1, score, masked_score)
        peak = jnp.max(score, axis=2, keepdims=True)
        weight = jnp.exp(score - peak)
        total = jnp.sum(weight, axis=2, keepdims=True)
        high = weight.astype(bf16)
        weight_high[:, at, :] = high
        weight_low[:, at, :] = (weight - high.astype(f32)).astype(bf16)
        peaks[:, at, :] = jnp.broadcast_to(peak, (heads, ROWS, lanes))
        sums[:, at, :] = jnp.broadcast_to(total, (heads, ROWS, lanes))
        blocks.append((at, own, other, high.reshape(heads * ROWS, keys), (1.0 / total).reshape(heads * ROWS, 1)))
    for at, own, other, flat, scale in blocks:
        own_part = jnp.where(diagonal, dot_nt(flat, own) * scale, 0.0).astype(bf16)
        other_part = jnp.where(diagonal, dot_nt(flat, other) * scale, 0.0).astype(bf16)
        pairs = dot(own_part, gather_own[...]) + dot(other_part, gather_other[...])
        part[0:heads, at, :] = pairs.reshape(heads, ROWS, lanes).astype(bf16)

    @pl.when(step == pl.num_programs(0) - 1)
    def _():
        own_frames = frames[pl.ds(pl.multiple_of(sub * half, half), half), :]
        lane = iota((half, 2 * SLOT), 1)
        first = lane < SLOT
        slot = lane % SLOT
        plane = (slot - CH) // PV
        inside = (slot >= CH) & (slot < CH + 3 * PV)

        def on_planes(columns):
            out = jnp.zeros((half, 2 * SLOT), f32)
            for b, column in columns:
                out = jnp.where(inside & (plane == b), own_frames[:, column : column + 1], out)
            return out

        shift = on_planes([(a, 9 + a) for a in range(3)])
        turns = [
            (d, on_planes([(b, 3 * (b - d) + b) for b in range(3) if 0 <= b - d < 3])) for d in range(-2, 3)
        ]
        for pair in range(heads // 2):
            a, b = 2 * pair, 2 * pair + 1
            left = jnp.concatenate([weight_high[a], weight_low[a], weight_high[b], weight_low[b]], axis=0)
            right = jnp.concatenate([values[a], values[b]], axis=0)
            out = dot_nt(left, right)
            upper = jnp.where(first, out[0:half], out[2 * half : 3 * half])
            lower = jnp.where(first, out[half : 2 * half], out[3 * half :])
            peak_pair = jnp.where(first, peaks[a], peaks[b])
            sum_pair = jnp.where(first, sums[a], sums[b])
            inverse = 1.0 / sum_pair
            points = (upper + lower + pltpu.roll(upper, 2 * SLOT - 3 * PV, 1)) * inverse - shift
            turned = jnp.zeros((half, 2 * SLOT), f32)
            for d, factor in turns:
                turned = turned + factor * (pltpu.roll(points, (d * PV) % (2 * SLOT), 1) if d else points)
            result = jnp.where(slot < CH, upper * inverse, turned)
            at = CH + 3 * PV
            for value in (peak_pair, sum_pair):
                for _ in range(3):
                    piece = rounded(value)
                    result = jnp.where(slot == at, piece, result)
                    value = value - piece
                    at += 1
            part[heads + pair] = jnp.where(slot < at, result, 0.0).astype(bf16)
        share = half // targets
        for target in range(targets):
            at = jnp.bitwise_xor(place[2], target) * share if targets > 1 else 0
            results[target][...] = part[:, pl.ds(pl.multiple_of(at, share) if targets > 1 else 0, share), :]


def attend(place, gains, inputs, key_blocks, own_pairs, other_pairs, mask, half, hidden, targets):
    channels, query_count, keys = own_pairs.shape
    features = inputs[0].shape[1]
    local_heads = gains[0].shape[0]
    heads = 2 * local_heads
    slots, lanes = heads + local_heads, 2 * channels
    rows = math.gcd(half, ATTEND_ROWS)
    steps = half // rows
    operands = [*inputs, *key_blocks]
    pair_block = pl.BlockSpec((channels, rows, keys), lambda g, p: (0, p[0] * steps + g, 0))
    return pl.pallas_call(
        functools.partial(attend_kernel, len(gains) + len(operands), len(key_blocks), targets),
        grid_spec=pltpu.PrefetchScalarGridSpec(
            num_scalar_prefetch=1,
            grid=(steps,),
            in_specs=[
                pair_block,
                pair_block,
                pl.BlockSpec((rows, keys), lambda g, p: (p[0] * steps + g, 0)),
                *[SMEM for _ in gains],
                *[whole(a) for a in operands],
            ],
            out_specs=[
                *[pl.BlockSpec((slots, half // targets, lanes), lambda g, p: (0, 0, 0))] * targets,
                pl.BlockSpec((hidden, keys), lambda g, p: (0, 0)),
            ],
            scratch_shapes=[
                pltpu.VMEM((slots, half, lanes), bf16),
                pltpu.VMEM((heads, half, keys), bf16),
                pltpu.VMEM((heads, half, keys), bf16),
                pltpu.VMEM((heads, half, lanes), f32),
                pltpu.VMEM((heads, half, lanes), f32),
                pltpu.VMEM((channels * ROWS, lanes), bf16),
                pltpu.VMEM((channels * ROWS, lanes), bf16),
                pltpu.VMEM((heads, half, keys), f32),
                pltpu.VMEM((heads, SLOT, keys), bf16),
                pltpu.VMEM((heads * ROWS, lanes * ROWS), bf16),
                pltpu.VMEM((query_count, 16), f32),
                pltpu.VMEM((keys, features), bf16),
                pltpu.VMEM((2, local_heads * KCOLS, keys), f32),
                pltpu.VMEM((2, local_heads * QCOLS, query_count), f32),
                pltpu.VMEM((heads, SLOT, keys), f32),
                pltpu.VMEM((heads, SLOT, query_count), f32),
                pltpu.VMEM((heads, query_count, SLOT), f32),
            ],
        ),
        out_shape=[
            *[jax.ShapeDtypeStruct((slots, half // targets, lanes), bf16)] * targets,
            jax.ShapeDtypeStruct((hidden, keys), f32),
        ],
        compiler_params=params(63),
        cost_estimate=cost(9),
        name="attend",
    )(place, own_pairs, other_pairs, mask, *gains, *operands)


def norm(values, gain):
    centred = values - jnp.mean(values, axis=-1, keepdims=True)
    variance = jnp.mean(centred * centred, axis=-1, keepdims=True)
    return centred * lax.rsqrt(variance + norm_epsilon) * gain


def node_kernel(
    count,
    place,
    nodes,
    out_own,
    out_other,
    first_gain,
    second_gain,
    gate_weight,
    up_weight,
    down_weight,
    *rest,
):
    parts, result = rest[:count], rest[count]
    *held, sems = rest[count + 1 :]
    sources = (out_own, out_other, gate_weight, up_weight, down_weight)
    loads = [pltpu.make_async_copy(a, b, sems.at[i]) for i, (a, b) in enumerate(zip(sources, held))]
    for load in loads:
        load.start()
    out_own, out_other, gate_weight, up_weight, down_weight = held
    heads = parts[0].shape[0] * 2 // 3
    rows, lanes = parts[0].shape[1:]
    local_heads = heads // 2
    tall = local_heads * rows
    first = iota((tall, lanes), 1) < SLOT
    slot = iota((tall, lanes), 1) % SLOT
    at = CH + 3 * PV

    def broadcast(values, lane):
        return jnp.where(
            first,
            jnp.broadcast_to(values[:, lane : lane + 1], (tall, lanes)),
            jnp.broadcast_to(values[:, SLOT + lane : SLOT + lane + 1], (tall, lanes)),
        )

    extras, peaks, sums = [], [], []
    for part in parts:
        extra = part[heads:].astype(f32).reshape(tall, lanes)
        joined = extra + pltpu.roll(extra, lanes - 1, 1) + pltpu.roll(extra, lanes - 2, 1)
        extras.append(extra)
        peaks.append(broadcast(joined, at))
        sums.append(broadcast(joined, at + 3))
    peak = functools.reduce(jnp.maximum, peaks)
    shares = [s * jnp.exp(p - peak) for s, p in zip(sums, peaks)]
    total = sum(shares)
    shares = [s / total for s in shares]
    merged = sum(s * e for s, e in zip(shares, extras))
    squares = merged * merged
    norms = jnp.sqrt(
        1.0 + pltpu.roll(squares, PV, 1) + pltpu.roll(squares, 2 * PV, 1) + pltpu.roll(squares, 3 * PV, 1)
    )
    merged = jnp.where(slot < at, merged, norms).astype(bf16)
    for load in loads[:2]:
        load.wait()
    projected = jnp.zeros((rows, nodes.shape[1]), f32)
    for head in range(heads):
        pair, odd = divmod(head, 2)
        weight = out_own if head < local_heads else out_other
        begin = (head % local_heads) * (FEATURES + lanes)
        span = slice(pair * rows, (pair + 1) * rows)
        lane = odd * SLOT
        mixed = jnp.zeros((rows, lanes), f32)
        for share, part in zip(shares, parts):
            factor = jnp.broadcast_to(share[span, lane : lane + 1], (rows, lanes))
            mixed = mixed + factor * part[head].astype(f32)
        projected = projected + dot(mixed.astype(bf16), weight[begin + FEATURES : begin + FEATURES + lanes])
        projected = projected + dot(merged[span, lane : lane + FEATURES], weight[begin : begin + FEATURES])
    own = nodes[pl.ds(pl.multiple_of(place[0], ROWS), rows), :]
    first_nodes = norm(own.astype(f32) + projected, first_gain[...])
    first_rounded = first_nodes.astype(bf16)
    for load in loads[2:]:
        load.wait()
    gate = dot(first_rounded, gate_weight[...])
    hidden = (gate / (1.0 + jnp.exp(-gate)) * dot(first_rounded, up_weight[...])).astype(bf16)
    result[...] = norm(first_nodes + dot(hidden, down_weight[...]), second_gain[...]).astype(bf16)


def update_nodes(place, parts, nodes, out_own, out_other, first_gain, second_gain, gate_weight, up_weight, down_weight):
    operands = [nodes, out_own, out_other, first_gain, second_gain, gate_weight, up_weight, down_weight, *parts]
    weights = [out_own, out_other, gate_weight, up_weight, down_weight]
    late = {1, 2, 5, 6, 7}
    hbm = pl.BlockSpec(memory_space=pl.ANY)
    return pl.pallas_call(
        functools.partial(node_kernel, len(parts)),
        in_specs=[SMEM] + [hbm if i in late else whole(a) for i, a in enumerate(operands)],
        scratch_shapes=[pltpu.VMEM(a.shape, bf16) for a in weights] + [pltpu.SemaphoreType.DMA((len(weights),))],
        out_shape=jax.ShapeDtypeStruct((parts[0].shape[1], nodes.shape[1]), bf16),
        compiler_params=params(16),
        cost_estimate=cost(2),
        name="nodes",
    )(place, *operands)


def turn_kernel(place, own_pairs, other_pairs, in_weight, out_weight, result, left, out_left):
    channels = own_pairs.shape[0]
    sub = place[0]

    @pl.when(pl.program_id(0) == 0)
    def _():
        own = pl.multiple_of(sub * channels, channels)
        other = pl.multiple_of((1 - sub) * channels, channels)
        left[:, 0:channels] = in_weight[pl.ds(own, channels), :].astype(f32).T.astype(bf16)
        left[:, channels:] = in_weight[pl.ds(other, channels), :].astype(f32).T.astype(bf16)
        flipped = out_weight[...].astype(f32).T
        out_left[0:channels] = jnp.where(sub == 0, flipped[0:channels], flipped[channels:]).astype(bf16)
        out_left[channels:] = jnp.where(sub == 0, flipped[channels:], flipped[0:channels]).astype(bf16)

    result[:, 0:channels, :] = jnp.swapaxes(own_pairs[...], 0, 1)
    result[:, channels:, :] = jnp.swapaxes(other_pairs[...], 0, 1)


def turn_pairs(place, own_pairs, other_pairs, in_weight, out_weight, half):
    channels, _, keys = other_pairs.shape
    both, hidden = in_weight.shape
    rows = math.gcd(half, TURN_ROWS)
    steps = half // rows
    return pl.pallas_call(
        turn_kernel,
        grid_spec=pltpu.PrefetchScalarGridSpec(
            num_scalar_prefetch=1,
            grid=(steps,),
            in_specs=[
                pl.BlockSpec((channels, rows, keys), lambda g, p: (0, p[0] * steps + g, 0)),
                pl.BlockSpec((channels, rows, keys), lambda g, p: (0, p[0] * steps + g, 0)),
                whole(in_weight),
                whole(out_weight),
            ],
            out_specs=(
                pl.BlockSpec((rows, both, keys), lambda g, p: (g, 0, 0)),
                pl.BlockSpec((hidden, both), lambda g, p: (0, 0)),
                pl.BlockSpec((both, hidden), lambda g, p: (0, 0)),
            ),
        ),
        out_shape=(
            jax.ShapeDtypeStruct((half, both, keys), bf16),
            jax.ShapeDtypeStruct((hidden, both), bf16),
            jax.ShapeDtypeStruct((both, hidden), bf16),
        ),
        compiler_params=params(16),
        cost_estimate=cost(4),
        name="turn_pairs",
    )(place, own_pairs, other_pairs, in_weight, out_weight)


def edge_kernel(count, place, turned, *rest):
    ring = rest[:count]
    edge_keys, in_left, out_left, query_weight, kept, sent, new_nodes, nodes, left, picks, hidden, fresh = rest[count:]
    step, rows = pl.program_id(0), ROWS
    _, both, keys = turned.shape
    channels = both // 2

    @pl.when(pl.program_id(0) == 0)
    def _():
        at = 0
        for source in ring:
            for begin in range(0, source.shape[0], rows):
                nodes[at] = source[begin : begin + rows]
                at += 1
        for span in range(left.shape[0]):
            left[span, :, 0:both] = in_left[...]
        chosen = iota((rows, 2 * rows, keys), 1) % rows == iota((rows, 2 * rows, keys), 0)
        picks[...] = chosen.astype(f32).astype(bf16)

    spans = turned.shape[0] // rows
    for span in range(spans):
        begin = span * rows
        own = nodes[jnp.bitwise_xor(step * spans + span, place[1])]
        queries = dot_tt(query_weight[...], own)
        high = queries.astype(bf16)
        left[span, :, both : both + rows] = high
        left[span, :, both + rows :] = (queries - high.astype(f32)).astype(bf16)
        new_nodes[begin : begin + rows] = own
        for at in range(sent.shape[0] - channels):
            sent[channels + at, begin : begin + rows] = own[:, at * keys : (at + 1) * keys]
    for row in range(spans * rows):
        right = jnp.concatenate([turned[row], picks[row % rows]], axis=0)
        hidden[row] = jnp.maximum(dot(left[row // rows], right) + edge_keys[...], 0.0).astype(bf16)
    for row in range(spans * rows):
        old = turned[row].astype(f32)
        fresh[row] = (old + dot(out_left[...], hidden[row])).astype(bf16)
    kept[...] = jnp.swapaxes(fresh[:, 0:channels, :], 0, 1)
    sent[0:channels] = jnp.swapaxes(fresh[:, channels:, :], 0, 1)


def update_pairs(place, count, turned, ring, edge_keys, in_left, out_left, query_weight):
    half, both, keys = turned.shape
    channels, hidden = both // 2, in_left.shape[0]
    rows, features = math.gcd(half, EDGE_ROWS), ring[0].shape[1]
    steps = half // rows
    assert features % keys == 0
    extra = features // keys
    return pl.pallas_call(
        functools.partial(edge_kernel, len(ring)),
        grid_spec=pltpu.PrefetchScalarGridSpec(
            num_scalar_prefetch=1,
            grid=(steps,),
            in_specs=[
                pl.BlockSpec((rows, both, keys), lambda g, p: (g, 0, 0)),
                *[whole(a) for a in ring],
                whole(edge_keys),
                whole(in_left),
                whole(out_left),
                whole(query_weight),
            ],
            out_specs=(
                pl.BlockSpec((channels, rows, keys), lambda g, p: (0, p[0] * steps + g, 0)),
                pl.BlockSpec((channels + extra, rows, keys), lambda g, p: (0, g, 0)),
                pl.BlockSpec((rows, features), lambda g, p: (p[0] * steps + g, 0)),
            ),
            scratch_shapes=[
                pltpu.VMEM((half // ROWS, ROWS, features), bf16),
                pltpu.VMEM((rows // ROWS, hidden, both + 2 * ROWS), bf16),
                pltpu.VMEM((ROWS, 2 * ROWS, keys), bf16),
                pltpu.VMEM((rows, hidden, keys), bf16),
                pltpu.VMEM((rows, both, keys), bf16),
            ],
        ),
        out_shape=(
            jax.ShapeDtypeStruct((channels, count, keys), bf16),
            jax.ShapeDtypeStruct((channels + extra, half, keys), bf16),
            jax.ShapeDtypeStruct((count, features), bf16),
        ),
        compiler_params=params(36),
        cost_estimate=cost(8),
        name="edges",
    )(place, turned, *ring, edge_keys, in_left, out_left, query_weight)


def finish_kernel(arrived, pairs_in, nodes_in, pairs, nodes, sems):
    channels, half, keys = pairs.shape[0], arrived.shape[1], arrived.shape[2]
    begin = pl.multiple_of((1 - lax.axis_index("sub")) * half, half)
    rows = pl.ds(begin, half)
    copies = [pltpu.make_async_copy(arrived.at[0:channels], pairs.at[:, rows, :], sems.at[0])]
    for at in range(arrived.shape[0] - channels):
        target = nodes.at[rows, at * keys : (at + 1) * keys]
        copies.append(pltpu.make_async_copy(arrived.at[channels + at], target, sems.at[1 + at]))
    for copy in copies:
        copy.start()
    for copy in copies:
        copy.wait()


def finish(arrived, pairs, nodes):
    hbm = pl.BlockSpec(memory_space=pl.ANY)
    return pl.pallas_call(
        finish_kernel,
        in_specs=[whole(arrived), hbm, hbm],
        out_specs=(hbm, hbm),
        out_shape=(
            jax.ShapeDtypeStruct(pairs.shape, bf16),
            jax.ShapeDtypeStruct(nodes.shape, bf16),
        ),
        scratch_shapes=[pltpu.SemaphoreType.DMA((1 + arrived.shape[0] - pairs.shape[0],))],
        input_output_aliases={1: 0, 2: 1},
        compiler_params=params(8),
        cost_estimate=cost(1),
        name="finish",
    )(arrived, pairs, nodes)


def shards(
    node_query,
    query_angles,
    query_trans,
    query_chain,
    node_key,
    key_angles,
    key_trans,
    key_chain,
    pair_features,
    pair_mask,
    query_weight,
    key_weight,
    bias_weight,
    point_gain,
    chain_gain,
    out_weight,
    first_gain,
    second_gain,
    gate_weight,
    up_weight,
    down_weight,
    edge_query_weight,
    edge_key_weight,
    edge_in_weight,
    edge_out_weight,
):
    subs, cols, rows = lax.axis_size("sub"), lax.axis_size("col"), lax.axis_size("row")
    sub, col = lax.axis_index("sub"), lax.axis_index("col")

    def swap(values):
        return lax.ppermute(values, "sub", [(i, (i + 1) % subs) for i in range(subs)])

    def step(by_row, by_sub):
        return [
            (r * subs + c, (r + by_row) % rows * subs + (c + by_sub) % subs) for r in range(rows) for c in range(subs)
        ]

    key_blocks = [node_key] + [
        lax.ppermute(node_key, ("row", "sub"), step(r, c)) for r in range(1, rows) for c in range(subs)
    ]
    half = node_query.shape[0] // subs
    query_weight, key_weight, bias_weight = query_weight.T, key_weight.T, bias_weight.T
    packed = pack(point_gain, chain_gain, key_weight, query_weight, bias_weight, node_key)
    packed = swap(packed)
    other_pairs = swap(pair_features)
    place = jnp.stack([sub, lax.axis_index("row"), col]).astype(jnp.int32)

    share = half // cols
    assert cols & (cols - 1) == 0
    spare = -share % ROWS
    targets = 1 if spare else cols
    *pieces, edge_keys = attend(
        place,
        [point_gain, chain_gain],
        [
            node_query,
            query_angles,
            query_trans,
            query_chain[None, :],
            key_angles,
            key_trans,
            key_chain[None, :],
            query_weight,
            key_weight,
            bias_weight,
            packed,
            edge_key_weight,
        ],
        key_blocks,
        pair_features,
        other_pairs,
        pair_mask,
        half,
        edge_key_weight.shape[1],
        targets,
    )
    other_out = swap(lax.optimization_barrier((out_weight, edge_keys))[0])
    if spare:
        pieces = [
            lax.dynamic_slice_in_dim(pieces[0], jnp.bitwise_xor(col, k) * share, share, 1) for k in range(cols)
        ]
    def meet(values, k):
        return lax.ppermute(values, "col", [(i, i ^ k) for i in range(cols)])

    order = range(cols - 1, 0, -1)
    met = {k: meet(pieces[k], k) for k in order}
    parts = [pieces[0]] + [met[k] for k in order]
    own_nodes, begin = node_query, sub * half + col * share
    if spare:
        own_nodes, begin = lax.dynamic_slice_in_dim(node_query, begin, share, 0), 0 * begin
        parts = [jnp.pad(p, ((0, 0), (0, spare), (0, 0))) for p in parts]
        own_nodes = jnp.pad(own_nodes, ((0, spare), (0, 0)))
    turn_place, _ = lax.optimization_barrier((place, pieces))
    turned, in_left, out_left = turn_pairs(
        turn_place, pair_features, other_pairs, edge_in_weight, edge_out_weight, half
    )
    own_nodes, turned = lax.optimization_barrier((own_nodes, turned))
    fresh_nodes = update_nodes(
        begin.astype(jnp.int32).reshape(1),
        parts,
        own_nodes,
        out_weight,
        other_out,
        first_gain[None, :],
        second_gain[None, :],
        gate_weight,
        up_weight,
        down_weight,
    )[:share]
    met = {k: meet(fresh_nodes, k) for k in order}
    ring = [fresh_nodes] + [met[k] for k in range(1, cols)]
    per_share = max(share // ROWS, 1)
    turn = col * per_share
    if spare:
        ring = [jnp.stack(ring)[jnp.bitwise_xor(jnp.arange(cols), col)].reshape(half, node_query.shape[1])]
        turn = 0 * col
    edge_place = jnp.stack([sub, turn]).astype(jnp.int32)
    kept, sent, new_nodes = update_pairs(
        edge_place, pair_features.shape[1], turned, ring, edge_keys, in_left, out_left, edge_query_weight
    )
    updated_pairs, updated_nodes = finish(swap(sent), kept, new_nodes)
    return (updated_nodes, updated_pairs)


def solution(mesh):
    return jax.shard_map(
        shards,
        mesh=mesh,
        in_specs=(
            P(("rep", "row"), None),
            P(None, ("rep", "row")),
            P(None, ("rep", "row")),
            P(("rep", "row")),
            P(("rep", "col", "row", "sub"), None),
            P(None, ("rep", "col")),
            P(None, ("rep", "col")),
            P(("rep", "col")),
            P("sub", ("rep", "row"), "col"),
            P(("rep", "row"), "col"),
            P(None, "sub"),
            P(None, "sub"),
            P(None, "sub"),
            P("sub"),
            P("sub"),
            P("sub", None),
            P(),
            P(),
            P(),
            P(),
            P(),
            P(),
            P(),
            P(),
            P(),
        ),
        out_specs=(P(("rep", "row"), None), P("sub", ("rep", "row"), "col")),
        check_vma=False,
    )
```
